32 devices in a mesh: dp: 4 (over y, x), ctx: 8 (over z, core).
Axes of the slice: x: 2, y: 2, z: 4, core: 2. Of those that a mesh axis runs over, the one named last changes fastest.
Arguments:
- inputs: bfloat16 [4, 16, 65536], P('dp', None, 'ctx'), may hold values from -6 to 6
- out_grad: bfloat16 [4, 16, 65536], P('dp', None, 'ctx'), may hold values from -0.0625 to 0.0625
- master: float32 [16, 65536], P('ctx', 'dp'), may hold values from -0.0234375 to 0.0234375
- moment_one: float32 [16, 65536], P('ctx', 'dp'), may hold values from -6 to 6
- moment_two: float32 [16, 65536], P('ctx', 'dp'), may hold values from 0.05 to 1
- next_inputs: bfloat16 [4, 16, 65536], P('dp', None, 'ctx'), may hold values from -6 to 6
Outputs:
- new_master: float32 [16, 65536], P('ctx', 'dp')
- new_moment_one: float32 [16, 65536], P('ctx', 'dp')
- new_moment_two: float32 [16, 65536], P('ctx', 'dp')
- next_out: bfloat16 [4, 16, 65536], P('dp', None, 'ctx')
The draws below stay inside these ranges and needn't reach their ends.
All inputs are finite; a program needn't handle non-finite values.
Results may differ from the reference program's by a relative error of at most 0.007.
Values may be sent and summed in bfloat16 or wider, within the bound.
A program may use at most 128 MiB of HBM per device.

```python
import math
import jax
import jax.numpy as jnp
from jax import lax

TAPS = 65536
CH = 16
DP = 4


def steps_of(rng, dims, pieces, least, largest):
    def one(dim, shards_of):
        steps = jax.random.uniform(jax.random.fold_in(jax.random.fold_in(rng, 6), dim), (shards_of,), jnp.float32, least / len(pieces), largest / len(pieces))
        return jnp.repeat(jnp.exp(steps), dims[dim] // shards_of).reshape((-1,) + (1,) * (len(dims) - dim - 1))

    factor_of = one(*pieces[0])
    for cut in pieces[1:]:
        factor_of = factor_of * one(*cut)
    return factor_of


def centred(stream_key, shape, deviation, reach, cuts=(), held_as=jnp.bfloat16):
    loudness = steps_of(stream_key, shape, cuts, -0.22, 0.18) if cuts else 1.0
    values = jax.random.normal(stream_key, shape, jnp.float32) * deviation * loudness
    return jnp.minimum(jnp.maximum(values, -reach), reach).astype(held_as)


def setup_inputs(seed: int = 0) -> dict:
    key_list = jax.random.split(jax.random.key(seed), 7)
    inputs = centred(key_list[0], (DP, CH, TAPS), 1.0, 6.0, ((0, 4), (2, 8)))
    out_grad = centred(key_list[1], (DP, CH, TAPS), (2.0 * (DP * TAPS) ** -0.5), 0.0625, ((0, 4), (2, 8)))
    master = centred(key_list[2], (CH, TAPS), TAPS ** -0.5, 0.0234375, ((0, 8), (1, 4)), jnp.float32)
    moment_one = centred(key_list[3], (CH, TAPS), 0.5, 6.0, ((0, 8), (1, 4)), jnp.float32)
    moment_two = jnp.clip(jnp.exp(math.log(1.0) - 2.9957323 * jax.random.uniform(key_list[4], (CH, TAPS), jnp.float32) ** steps_of(key_list[4], (CH, TAPS), ((0, 8), (1, 4)), -0.2, 0.2)), 0.05, 1.0)
    next_inputs = centred(key_list[5], (DP, CH, TAPS), 1.0, 6.0, ((0, 4), (2, 8)))
    return dict(inputs=inputs, out_grad=out_grad, master=master, moment_one=moment_one, moment_two=moment_two, next_inputs=next_inputs)


def reference(inputs, out_grad, master, moment_one, moment_two, next_inputs):
    length = 2 * TAPS
    seq_spec = jnp.fft.rfft(inputs.astype(jnp.float32), n=length, axis=-1)
    grad_spec = jnp.fft.rfft(out_grad.astype(jnp.float32), n=length, axis=-1)
    corr = jnp.fft.irfft(jnp.conj(seq_spec) * grad_spec, n=length, axis=-1)[..., :TAPS]
    grad = lax.optimization_barrier(jnp.sum(corr, axis=0))
    new_one = 0.9 * moment_one + 0.1 * grad
    new_two = 0.999 * moment_two + 0.001 * grad * grad
    first_hat = new_one / (1.0 - 0.9 ** 10)
    second_hat = new_two / (1.0 - 0.999 ** 10)
    new_master = master - 0.01 * (first_hat / (jnp.sqrt(second_hat) + 1e-08) + 0.1 * master)
    filters = new_master.astype(jnp.bfloat16).astype(jnp.float32)
    filter_spec = jnp.fft.rfft(filters, n=length, axis=-1)
    next_spec = jnp.fft.rfft(next_inputs.astype(jnp.float32), n=length, axis=-1)
    result = jnp.fft.irfft(next_spec * filter_spec[None], n=length, axis=-1)[..., :TAPS]
    return (new_master, new_one, new_two, result.astype(jnp.bfloat16))
```

```python
import functools

import jax
import jax.numpy as jnp
import numpy as np
from jax import lax
from jax.experimental import pallas as pl
from jax.experimental.pallas import tpu as pltpu
from jax.sharding import PartitionSpec as P

F32 = jnp.float32
BF16 = jnp.bfloat16
MESH = pl.DeviceIdType.MESH


def split_table(table):
    high = table.astype(np.float32).astype(jnp.bfloat16)
    low = (table - high.astype(np.float64)).astype(np.float32).astype(jnp.bfloat16)
    return high, low


def tables(rows, cols):
    length = rows * cols
    shifted = np.arange(rows, dtype=np.float64) + 0.25
    first = 2.0 * np.pi * np.outer(shifted, np.arange(rows)) / rows
    turn = 2.0 * np.pi * np.outer(shifted, np.arange(cols)) / length
    second = 2.0 * np.pi * (np.outer(np.arange(cols), np.arange(cols)) % cols) / cols
    in_first = np.concatenate([np.cos(first), -np.sin(first)], 0)
    out_last = np.concatenate([np.cos(first).T, -np.sin(first).T], 1) / length
    cosine, sine = np.cos(second), np.sin(second)
    forward = np.block([[cosine, -sine], [sine, cosine]])
    back = np.block([[cosine, sine], [-sine, cosine]])
    return (
        np.stack(split_table(in_first)),
        np.stack([np.cos(turn), -np.sin(turn)]).astype(np.float32),
        np.stack(split_table(forward)),
        np.stack(split_table(back)),
        np.stack(split_table(out_last)),
    )


def dot(left, right):
    return jnp.dot(left, right, preferred_element_type=F32)


def halves(value):
    high = value.astype(BF16)
    return high, (value - high.astype(F32)).astype(BF16)


def forward(block, t_first, t_turn, t_forward):
    rows, cols = block.shape
    mixed = dot(t_first[0], block) + dot(t_first[1], block)
    real, imag = mixed[:rows], mixed[rows:]
    turn_re, turn_im = t_turn[0], t_turn[1]
    turned = jnp.concatenate(
        [real * turn_re - imag * turn_im, real * turn_im + imag * turn_re], axis=1
    )
    high, low = halves(turned)
    spec = dot(high, t_forward[0]) + dot(low, t_forward[0]) + dot(high, t_forward[1])
    return spec[:, :cols], spec[:, cols:]


def inverse(real, imag, t_turn, t_back, t_last):
    cols = real.shape[1]
    high, low = halves(jnp.concatenate([real, imag], axis=1))
    mixed = dot(high, t_back[0]) + dot(low, t_back[0]) + dot(high, t_back[1])
    real, imag = mixed[:, :cols], mixed[:, cols:]
    turn_re, turn_im = t_turn[0], t_turn[1]
    high, low = halves(
        jnp.concatenate([real * turn_re + imag * turn_im, imag * turn_re - real * turn_im], axis=0)
    )
    return dot(t_last[0], high) + dot(t_last[0], low) + dot(t_last[1], high)


def layer(
    n_dp,
    n_ctx,
    x_hbm,
    g_hbm,
    master_hbm,
    one_hbm,
    two_hbm,
    n_hbm,
    first_hbm,
    turn_hbm,
    forward_hbm,
    back_hbm,
    last_hbm,
    master_out,
    one_out,
    two_out,
    next_out,
    raw,
    block_send,
    block_recv,
    t_first,
    t_turn,
    t_forward,
    t_back,
    t_last,
    state_in,
    state,
    state_out,
    spec,
    partial,
    grad_send,
    grad_recv,
    filt,
    out_send,
    out_recv,
    out_flat,
    local_sem,
    store_sem,
    block_ssem,
    block_rsem,
    grad_ssem,
    grad_rsem,
    filt_ssem,
    filt_rsem,
    out_ssem,
    out_rsem,
):
    me_dp = lax.axis_index("dp")
    me = lax.axis_index("ctx")
    channels = raw.shape[1]
    owned = block_recv.shape[1]
    rows_block, cols = block_send.shape[2:]
    rows = n_ctx * rows_block
    rows_own = filt.shape[2]

    barrier = pltpu.get_barrier_semaphore()

    def greet_ctx(i, carry):
        peer = lax.rem(me + i, n_ctx)
        pl.semaphore_signal(barrier, inc=1, device_id={"ctx": peer}, device_id_type=MESH)
        return carry

    def greet_dp(i, carry):
        peer = lax.rem(me_dp + i, n_dp)
        pl.semaphore_signal(barrier, inc=1, device_id={"dp": peer}, device_id_type=MESH)
        return carry

    lax.fori_loop(1, n_ctx, greet_ctx, 0)
    lax.fori_loop(1, n_dp, greet_dp, 0)

    loads = []
    for source, target in (
        (x_hbm.at[0], raw.at[0]),
        (g_hbm.at[0], raw.at[1]),
        (first_hbm, t_first),
        (turn_hbm, t_turn),
        (forward_hbm, t_forward),
        (back_hbm, t_back),
        (last_hbm, t_last),
        (n_hbm.at[0], raw.at[2]),
        (master_hbm, state_in.at[0]),
        (one_hbm, state_in.at[1]),
        (two_hbm, state_in.at[2]),
    ):
        copy = pltpu.make_async_copy(source, target, local_sem.at[len(loads)])
        copy.start()
        loads.append(copy)

    def regroup(which):
        block_send[which] = (
            raw[which].astype(F32).reshape(channels, rows_block, cols).astype(BF16)
        )

    def send_block(which, ch):
        def one(i, carry):
            peer = lax.rem(me + i, n_ctx)
            pltpu.make_async_remote_copy(
                src_ref=block_send.at[which, peer * owned + ch],
                dst_ref=block_recv.at[which, ch, me],
                send_sem=block_ssem.at[which, ch],
                recv_sem=block_rsem.at[which, ch],
                device_id={"ctx": peer},
                device_id_type=MESH,
            ).start()
            return carry

        lax.fori_loop(1, n_ctx, one, 0)
        block_recv[which, ch, me] = block_send[which, me * owned + ch]

    def wait_bytes(ref, count, sem):
        part = ref.at[pl.ds(0, count)]
        pltpu.make_async_copy(part, part, sem).wait()

    def wait_block(which, ch):
        wait_bytes(block_recv.at[which, ch], n_ctx - 1, block_rsem.at[which, ch])
        return block_recv[which, ch].reshape(rows, cols)

    def spectrum(block):
        return forward(block, t_first, t_turn, t_forward)

    loads[0].wait()
    regroup(0)
    pl.semaphore_wait(barrier, n_ctx + n_dp - 2)
    send_block(0, 0)
    loads[1].wait()
    regroup(1)
    send_block(1, 0)
    for ch in range(1, owned):
        send_block(0, ch)
        send_block(1, ch)
    for copy in loads[2:]:
        copy.wait()
    regroup(2)
    for which in range(3):
        for ch in range(owned):
            state[which, ch] = state_in[which, ch : ch + 1, :].reshape(rows_own, cols)

    def gradient(ch):
        spec[0], spec[1] = spectrum(wait_block(0, ch))
        g_block = wait_block(1, ch)
        if ch == owned - 1:
            for later in range(owned):
                send_block(2, later)
        g_re, g_im = spectrum(g_block)
        x_re, x_im = spec[0], spec[1]
        total = inverse(
            x_re * g_re + x_im * g_im, x_re * g_im - x_im * g_re, t_turn, t_back, t_last
        ).reshape(n_dp, rows_own, cols)
        partial[ch] = total
        grad_send[ch] = total.astype(BF16)

        def one(i, carry):
            peer = lax.rem(me_dp + i, n_dp)
            pltpu.make_async_remote_copy(
                src_ref=grad_send.at[ch, peer],
                dst_ref=grad_recv.at[ch, i - 1],
                send_sem=grad_ssem.at[ch],
                recv_sem=grad_rsem.at[ch],
                device_id={"dp": peer},
                device_id_type=MESH,
            ).start()
            return carry

        lax.fori_loop(1, n_dp, one, 0)

    def update(ch):
        wait_bytes(grad_recv.at[ch], n_dp - 1, grad_rsem.at[ch])
        grad = partial[ch, me_dp]
        for i in range(n_dp - 1):
            grad = grad + grad_recv[ch, i].astype(F32)
        master = state[0, ch]
        new_one = 0.9 * state[1, ch] + 0.1 * grad
        new_two = 0.999 * state[2, ch] + 0.001 * grad * grad
        first_hat = new_one / (1.0 - 0.9**10)
        second_hat = new_two / (1.0 - 0.999**10)
        new_master = master - 0.01 * (first_hat / (jnp.sqrt(second_hat) + 1e-08) + 0.1 * master)
        filt[ch, me_dp] = new_master.astype(BF16)

        def one(i, carry):
            peer = lax.rem(me_dp + i, n_dp)
            pltpu.make_async_remote_copy(
                src_ref=filt.at[ch, me_dp],
                dst_ref=filt.at[ch, me_dp],
                send_sem=filt_ssem.at[ch],
                recv_sem=filt_rsem.at[ch],
                device_id={"dp": peer},
                device_id_type=MESH,
            ).start()
            return carry

        lax.fori_loop(1, n_dp, one, 0)
        for which, value in enumerate((new_master, new_one, new_two)):
            state_out[which, ch : ch + 1, :] = value.reshape(1, rows_own * cols)

    def following(ch):
        spec[0], spec[1] = spectrum(wait_block(2, ch))
        wait_bytes(filt.at[ch], n_dp - 1, filt_rsem.at[ch])
        f_re, f_im = spectrum(filt[ch].reshape(rows, cols))
        x_re, x_im = spec[0], spec[1]
        result = inverse(
            x_re * f_re - x_im * f_im, x_re * f_im + x_im * f_re, t_turn, t_back, t_last
        )
        out_send[ch] = result.astype(BF16).reshape(n_ctx, rows_block, cols)

        def one(i, carry):
            peer = lax.rem(me + i, n_ctx)
            pltpu.make_async_remote_copy(
                src_ref=out_send.at[ch, peer],
                dst_ref=out_recv.at[me * owned + ch],
                send_sem=out_ssem.at[ch],
                recv_sem=out_rsem.at[ch],
                device_id={"ctx": peer},
                device_id_type=MESH,
            ).start()
            return carry

        lax.fori_loop(1, n_ctx, one, 0)
        out_recv[me * owned + ch] = out_send[ch, me]

    for ch in range(owned):
        gradient(ch)
        if ch:
            update(ch - 1)
    update(owned - 1)
    stores = []
    for which, target in enumerate((master_out, one_out, two_out)):
        copy = pltpu.make_async_copy(state_out.at[which], target, store_sem.at[which])
        copy.start()
        stores.append(copy)
    for ch in range(owned):
        following(ch)
    for ch in range(owned):
        wait_bytes(out_recv, n_ctx - 1, out_rsem.at[ch])
    out_flat[...] = out_recv[...].astype(F32).reshape(channels, rows_block * cols).astype(BF16)
    copy = pltpu.make_async_copy(out_flat, next_out.at[0], store_sem.at[3])
    copy.start()
    stores.append(copy)
    for ch in range(owned):
        for which in range(3):
            wait_bytes(block_send.at[which], n_ctx - 1, block_ssem.at[which, ch])
        wait_bytes(grad_send.at[ch], n_dp - 1, grad_ssem.at[ch])
        wait_bytes(filt.at[ch], n_dp - 1, filt_ssem.at[ch])
        wait_bytes(out_send.at[ch], n_ctx - 1, out_ssem.at[ch])
    for copy in stores:
        copy.wait()


def local(n_dp, n_ctx, inputs, out_grad, master, moment_one, moment_two, next_inputs):
    channels, span = inputs.shape[1:]
    owned, taps_own = master.shape
    length = n_ctx * span
    cols = min(256, span // 16)
    rows = length // cols
    rows_block, rows_own = span // cols, taps_own // cols
    table_list = tables(rows, cols)
    dma = pltpu.SemaphoreType.DMA
    vmem = pltpu.VMEM
    anywhere = pl.BlockSpec(memory_space=pl.ANY)
    macs = 12 * owned * length * (rows + 2 * cols) * 3
    return pl.pallas_call(
        functools.partial(layer, n_dp, n_ctx),
        name="layer",
        out_shape=(
            jax.ShapeDtypeStruct(master.shape, F32),
            jax.ShapeDtypeStruct(master.shape, F32),
            jax.ShapeDtypeStruct(master.shape, F32),
            jax.ShapeDtypeStruct(inputs.shape, BF16),
        ),
        in_specs=[anywhere] * 11,
        out_specs=[anywhere] * 4,
        scratch_shapes=[
            vmem((3, channels, span), BF16),
            vmem((3, channels, rows_block, cols), BF16),
            vmem((3, owned, n_ctx, rows_block, cols), BF16),
            *[vmem(table.shape, table.dtype) for table in table_list],
            vmem((3, owned, taps_own), F32),
            vmem((3, owned, rows_own, cols), F32),
            vmem((3, owned, taps_own), F32),
            vmem((2, rows, cols), F32),
            vmem((owned, n_dp, rows_own, cols), F32),
            vmem((owned, n_dp, rows_own, cols), BF16),
            vmem((owned, n_dp - 1, rows_own, cols), BF16),
            vmem((owned, n_dp, rows_own, cols), BF16),
            vmem((owned, n_ctx, rows_block, cols), BF16),
            vmem((channels, rows_block, cols), BF16),
            vmem((channels, span), BF16),
            dma((11,)),
            dma((4,)),
            dma((3, owned)),
            dma((3, owned)),
            dma((owned,)),
            dma((owned,)),
            dma((owned,)),
            dma((owned,)),
            dma((owned,)),
            dma((owned,)),
        ],
        compiler_params=pltpu.CompilerParams(
            collective_id=0, has_side_effects=True, vmem_limit_bytes=40 * 1024 * 1024
        ),
        cost_estimate=pl.CostEstimate(
            flops=2 * macs, bytes_accessed=8 * 1024 * 1024, transcendentals=0
        ),
    )(inputs, out_grad, master, moment_one, moment_two, next_inputs, *table_list)


def solution(mesh):
    return jax.shard_map(
        functools.partial(local, mesh.shape["dp"], mesh.shape["ctx"]),
        mesh=mesh,
        in_specs=(
            P("dp", None, "ctx"),
            P("dp", None, "ctx"),
            P("ctx", "dp"),
            P("ctx", "dp"),
            P("ctx", "dp"),
            P("dp", None, "ctx"),
        ),
        out_specs=(P("ctx", "dp"), P("ctx", "dp"), P("ctx", "dp"), P("dp", None, "ctx")),
        check_vma=False,
    )
```

```python
import functools

import jax
import jax.numpy as jnp
import numpy as np
from jax import lax
from jax.experimental import pallas as pl
from jax.experimental.pallas import tpu as pltpu
from jax.sharding import PartitionSpec as P

F32 = jnp.float32
BF16 = jnp.bfloat16
MESH = pl.DeviceIdType.MESH


def tables(rows, cols):
    length = rows * cols
    shifted = np.arange(rows, dtype=np.float64) + 0.25
    first = 2.0 * np.pi * np.outer(shifted, np.arange(rows)) / rows
    turn = 2.0 * np.pi * np.outer(shifted, np.arange(cols)) / length
    second = 2.0 * np.pi * (np.outer(np.arange(cols), np.arange(cols)) % cols) / cols
    return tuple(
        table.astype(np.float32)
        for table in (
            np.concatenate([np.cos(first), -np.sin(first)], 0),
            np.stack([np.cos(turn), -np.sin(turn)]),
            np.stack([np.cos(second), np.sin(second)]),
            np.concatenate([np.cos(first).T, -np.sin(first).T], 1) / length,
        )
    )


def dot(left, right):
    return jnp.dot(left, right, preferred_element_type=F32)


def halves(value):
    high = value.astype(BF16)
    return high, (value - high.astype(F32)).astype(BF16)


def forward(block, t_first, t_turn, t_forward):
    rows, cols = block.shape
    mixed = dot(t_first[0], block) + dot(t_first[1], block)
    real, imag = mixed[:rows], mixed[rows:]
    turn_re, turn_im = t_turn[0], t_turn[1]
    turned = jnp.concatenate(
        [real * turn_re - imag * turn_im, real * turn_im + imag * turn_re], axis=1
    )
    high, low = halves(turned)
    spec = dot(high, t_forward[0]) + dot(low, t_forward[0]) + dot(high, t_forward[1])
    return spec[:, :cols], spec[:, cols:]


def inverse(real, imag, t_turn, t_back, t_last):
    cols = real.shape[1]
    high, low = halves(jnp.concatenate([real, imag], axis=1))
    mixed = dot(high, t_back[0]) + dot(low, t_back[0]) + dot(high, t_back[1])
    real, imag = mixed[:, :cols], mixed[:, cols:]
    turn_re, turn_im = t_turn[0], t_turn[1]
    high, low = halves(
        jnp.concatenate([real * turn_re + imag * turn_im, imag * turn_re - real * turn_im], axis=0)
    )
    return dot(t_last[0], high) + dot(t_last[0], low) + dot(t_last[1], high)


def layer(
    n_dp,
    n_ctx,
    x_hbm,
    g_hbm,
    master_hbm,
    one_hbm,
    two_hbm,
    n_hbm,
    first_hbm,
    turn_hbm,
    second_hbm,
    last_hbm,
    master_out,
    one_out,
    two_out,
    out_recv,
    raw,
    block_send,
    block_recv,
    w_first,
    t_turn,
    w_second,
    w_last,
    t_first,
    t_forward,
    t_back,
    t_last,
    state_in,
    state,
    state_out,
    spec,
    partial,
    grad_send,
    grad_recv,
    filt,
    out_send,
    local_sem,
    store_sem,
    block_ssem,
    block_rsem,
    grad_ssem,
    grad_rsem,
    filt_ssem,
    filt_rsem,
    out_ssem,
    out_rsem,
):
    me_dp = lax.axis_index("dp")
    me = lax.axis_index("ctx")
    channels = raw.shape[1]
    owned = block_recv.shape[1]
    rows_block, cols = block_send.shape[2:]
    rows = n_ctx * rows_block
    rows_own = filt.shape[2]

    barrier = pltpu.get_barrier_semaphore()

    def greet_ctx(i, carry):
        peer = lax.rem(me + i, n_ctx)
        pl.semaphore_signal(barrier, inc=1, device_id={"ctx": peer}, device_id_type=MESH)
        return carry

    def greet_dp(i, carry):
        peer = lax.rem(me_dp + i, n_dp)
        pl.semaphore_signal(barrier, inc=1, device_id={"dp": peer}, device_id_type=MESH)
        return carry

    lax.fori_loop(1, n_ctx, greet_ctx, 0)
    lax.fori_loop(1, n_dp, greet_dp, 0)

    loads = []
    for source, target in (
        (x_hbm.at[0], raw.at[0]),
        (g_hbm.at[0], raw.at[1]),
        (first_hbm, w_first),
        (turn_hbm, t_turn),
        (second_hbm, w_second),
        (last_hbm, w_last),
        (n_hbm.at[0], raw.at[2]),
        (master_hbm, state_in.at[0]),
        (one_hbm, state_in.at[1]),
        (two_hbm, state_in.at[2]),
    ):
        copy = pltpu.make_async_copy(source, target, local_sem.at[len(loads)])
        copy.start()
        loads.append(copy)

    def regroup(which):
        block_send[which] = (
            raw[which].astype(F32).reshape(channels, rows_block, cols).astype(BF16)
        )

    def send_block(which, ch):
        def one(i, carry):
            peer = lax.rem(me + i, n_ctx)
            pltpu.make_async_remote_copy(
                src_ref=block_send.at[which, peer * owned + ch],
                dst_ref=block_recv.at[which, ch, me],
                send_sem=block_ssem.at[which, ch],
                recv_sem=block_rsem.at[which, ch],
                device_id={"ctx": peer},
                device_id_type=MESH,
            ).start()
            return carry

        lax.fori_loop(1, n_ctx, one, 0)
        block_recv[which, ch, me] = block_send[which, me * owned + ch]

    def wait_bytes(ref, count, sem):
        part = ref.at[pl.ds(0, count)]
        pltpu.make_async_copy(part, part, sem).wait()

    def wait_block(which, ch):
        wait_bytes(block_recv.at[which, ch], n_ctx - 1, block_rsem.at[which, ch])
        return block_recv[which, ch].reshape(rows, cols)

    def spectrum(block):
        return forward(block, t_first, t_turn, t_forward)

    loads[0].wait()
    regroup(0)
    pl.semaphore_wait(barrier, n_ctx + n_dp - 2)
    send_block(0, 0)
    loads[1].wait()
    regroup(1)
    send_block(1, 0)
    for ch in range(1, owned):
        send_block(0, ch)
        send_block(1, ch)
    for copy in loads[2:]:
        copy.wait()
    t_first[0], t_first[1] = halves(w_first[...])
    t_last[0], t_last[1] = halves(w_last[...])
    low_cols, high_cols = slice(0, cols), slice(cols, 2 * cols)
    for part, (cosine, sine) in enumerate(zip(halves(w_second[0]), halves(w_second[1]))):
        for table, upper, lower in ((t_forward, -sine, sine), (t_back, sine, -sine)):
            table[part, low_cols, low_cols] = cosine
            table[part, low_cols, high_cols] = upper
            table[part, high_cols, low_cols] = lower
            table[part, high_cols, high_cols] = cosine
    regroup(2)
    for which in range(3):
        for ch in range(owned):
            state[which, ch] = state_in[which, ch : ch + 1, :].reshape(rows_own, cols)

    def keep(values):
        spec[0], spec[1] = values

    def gradient(ch):
        g_block = wait_block(1, ch)
        if ch == owned - 1:
            for later in range(owned):
                send_block(2, later)
        g_re, g_im = spectrum(g_block)
        x_re, x_im = spec[0], spec[1]
        total = inverse(
            x_re * g_re + x_im * g_im, x_re * g_im - x_im * g_re, t_turn, t_back, t_last
        ).reshape(n_dp, rows_own, cols)
        partial[ch] = total
        grad_send[ch] = total.astype(BF16)

        def one(i, carry):
            peer = lax.rem(me_dp + i, n_dp)
            pltpu.make_async_remote_copy(
                src_ref=grad_send.at[ch, peer],
                dst_ref=grad_recv.at[ch, i - 1],
                send_sem=grad_ssem.at[ch],
                recv_sem=grad_rsem.at[ch],
                device_id={"dp": peer},
                device_id_type=MESH,
            ).start()
            return carry

        lax.fori_loop(1, n_dp, one, 0)

    def update(ch):
        wait_bytes(grad_recv.at[ch], n_dp - 1, grad_rsem.at[ch])
        grad = partial[ch, me_dp]
        for i in range(n_dp - 1):
            grad = grad + grad_recv[ch, i].astype(F32)
        master = state[0, ch]
        new_one = 0.9 * state[1, ch] + 0.1 * grad
        new_two = 0.999 * state[2, ch] + 0.001 * grad * grad
        first_hat = new_one / (1.0 - 0.9**10)
        second_hat = new_two / (1.0 - 0.999**10)
        new_master = master - 0.01 * (first_hat / (jnp.sqrt(second_hat) + 1e-08) + 0.1 * master)
        filt[ch, me_dp] = new_master.astype(BF16)

        def one(i, carry):
            peer = lax.rem(me_dp + i, n_dp)
            pltpu.make_async_remote_copy(
                src_ref=filt.at[ch, me_dp],
                dst_ref=filt.at[ch, me_dp],
                send_sem=filt_ssem.at[ch],
                recv_sem=filt_rsem.at[ch],
                device_id={"dp": peer},
                device_id_type=MESH,
            ).start()
            return carry

        lax.fori_loop(1, n_dp, one, 0)
        for which, value in enumerate((new_master, new_one, new_two)):
            state_out[which, ch : ch + 1, :] = value.reshape(1, rows_own * cols)

    def product(ch):
        wait_bytes(filt.at[ch], n_dp - 1, filt_rsem.at[ch])
        f_re, f_im = spectrum(filt[ch].reshape(rows, cols))
        x_re, x_im = spec[0], spec[1]
        keep((x_re * f_re - x_im * f_im, x_re * f_im + x_im * f_re))

    def finish(ch):
        result = inverse(spec[0], spec[1], t_turn, t_back, t_last)
        out_send[ch] = result.astype(BF16).reshape(n_ctx, rows_block, cols)

        def one(i, carry):
            peer = lax.rem(me + i, n_ctx)
            pltpu.make_async_remote_copy(
                src_ref=out_send.at[ch, peer],
                dst_ref=out_recv.at[me * owned + ch],
                send_sem=out_ssem.at[ch],
                recv_sem=out_rsem.at[ch],
                device_id={"ctx": peer},
                device_id_type=MESH,
            ).start()
            return carry

        lax.fori_loop(1, n_ctx, one, 0)
        copy = pltpu.make_async_copy(
            out_send.at[ch, me], out_recv.at[me * owned + ch], local_sem.at[ch]
        )
        copy.start()
        stores.append(copy)

    stores = []
    for ch in range(owned):
        keep(spectrum(wait_block(0, ch)))
        if ch:
            update(ch - 1)
        gradient(ch)
    final = owned - 1
    for ch in range(final):
        keep(spectrum(wait_block(2, ch)))
        product(ch)
        if ch == final - 1:
            update(final)
        finish(ch)
    if not final:
        update(final)
    keep(spectrum(wait_block(2, final)))
    product(final)
    for which, target in enumerate((master_out, one_out, two_out)):
        copy = pltpu.make_async_copy(state_out.at[which], target, store_sem.at[which])
        copy.start()
        stores.append(copy)
    finish(final)
    for ch in range(owned):
        for which in range(3):
            wait_bytes(block_send.at[which], n_ctx - 1, block_ssem.at[which, ch])
        wait_bytes(grad_send.at[ch], n_dp - 1, grad_ssem.at[ch])
        wait_bytes(filt.at[ch], n_dp - 1, filt_ssem.at[ch])
        wait_bytes(out_send.at[ch], n_ctx - 1, out_ssem.at[ch])
    for ch in range(owned):
        wait_bytes(out_recv, n_ctx - 1, out_rsem.at[ch])
    for copy in stores:
        copy.wait()


def settle(states, blocks, states_out, next_out, block, flat, sems):
    copies = [
        pltpu.make_async_copy(source, target, sems.at[i])
        for i, (source, target) in enumerate(zip(states, states_out))
    ]
    load = pltpu.make_async_copy(blocks, block, sems.at[3])
    load.start()
    for copy in copies:
        copy.start()
    load.wait()
    flat[...] = block[...].astype(F32).reshape(flat.shape).astype(BF16)
    store = pltpu.make_async_copy(flat, next_out.at[0], sems.at[4])
    store.start()
    store.wait()
    for copy in copies:
        copy.wait()


def settle_kernel(master, one, two, blocks, master_out, one_out, two_out, next_out, *scratch):
    settle((master, one, two), blocks, (master_out, one_out, two_out), next_out, *scratch)


def local(n_dp, n_ctx, inputs, out_grad, master, moment_one, moment_two, next_inputs):
    channels, span = inputs.shape[1:]
    owned, taps_own = master.shape
    length = n_ctx * span
    cols = min(256, span // 16)
    rows = length // cols
    rows_block, rows_own = span // cols, taps_own // cols
    table_list = tables(rows, cols)
    dma = pltpu.SemaphoreType.DMA
    vmem = pltpu.VMEM
    anywhere = pl.BlockSpec(memory_space=pltpu.HBM)
    macs = 12 * owned * length * (rows + 2 * cols) * 3
    results = pl.pallas_call(
        functools.partial(layer, n_dp, n_ctx),
        name="layer",
        out_shape=(
            jax.ShapeDtypeStruct(master.shape, F32),
            jax.ShapeDtypeStruct(master.shape, F32),
            jax.ShapeDtypeStruct(master.shape, F32),
            jax.ShapeDtypeStruct((channels, rows_block, cols), BF16),
        ),
        in_specs=[anywhere] * 10,
        out_specs=[anywhere] * 4,
        scratch_shapes=[
            vmem((3, channels, span), BF16),
            vmem((3, channels, rows_block, cols), BF16),
            vmem((3, owned, n_ctx, rows_block, cols), BF16),
            *[vmem(table.shape, F32) for table in table_list],
            vmem((2, 2 * rows, rows), BF16),
            vmem((2, 2 * cols, 2 * cols), BF16),
            vmem((2, 2 * cols, 2 * cols), BF16),
            vmem((2, rows, 2 * rows), BF16),
            vmem((3, owned, taps_own), F32),
            vmem((3, owned, rows_own, cols), F32),
            vmem((3, owned, taps_own), F32),
            vmem((2, rows, cols), F32),
            vmem((owned, n_dp, rows_own, cols), F32),
            vmem((owned, n_dp, rows_own, cols), BF16),
            vmem((owned, n_dp - 1, rows_own, cols), BF16),
            vmem((owned, n_dp, rows_own, cols), BF16),
            vmem((owned, n_ctx, rows_block, cols), BF16),
            dma((10,)),
            dma((3,)),
            dma((3, owned)),
            dma((3, owned)),
            dma((owned,)),
            dma((owned,)),
            dma((owned,)),
            dma((owned,)),
            dma((owned,)),
            dma((owned,)),
        ],
        compiler_params=pltpu.CompilerParams(
            collective_id=0, has_side_effects=True, vmem_limit_bytes=56 * 1024 * 1024
        ),
        cost_estimate=pl.CostEstimate(
            flops=2 * macs, bytes_accessed=8 * 1024 * 1024, transcendentals=0
        ),
    )(inputs, out_grad, master, moment_one, moment_two, next_inputs, *table_list)
    return pl.pallas_call(
        settle_kernel,
        name="settle",
        out_shape=(
            jax.ShapeDtypeStruct(master.shape, F32),
            jax.ShapeDtypeStruct(master.shape, F32),
            jax.ShapeDtypeStruct(master.shape, F32),
            jax.ShapeDtypeStruct(inputs.shape, BF16),
        ),
        in_specs=[anywhere] * 4,
        out_specs=[anywhere] * 4,
        scratch_shapes=[
            vmem((channels, rows_block, cols), BF16),
            vmem((channels, span), BF16),
            dma((5,)),
        ],
        compiler_params=pltpu.CompilerParams(vmem_limit_bytes=56 * 1024 * 1024),
    )(*results)


def solution(mesh):
    return jax.shard_map(
        functools.partial(local, mesh.shape["dp"], mesh.shape["ctx"]),
        mesh=mesh,
        in_specs=(
            P("dp", None, "ctx"),
            P("dp", None, "ctx"),
            P("ctx", "dp"),
            P("ctx", "dp"),
            P("ctx", "dp"),
            P("dp", None, "ctx"),
        ),
        out_specs=(P("ctx", "dp"), P("ctx", "dp"), P("ctx", "dp"), P("dp", None, "ctx")),
        check_vma=False,
    )
```

```python
import functools

import jax
import jax.numpy as jnp
import numpy as np
from jax import lax
from jax.experimental import pallas as pl
from jax.experimental.pallas import tpu as pltpu
from jax.sharding import PartitionSpec as P

F32 = jnp.float32
BF16 = jnp.bfloat16
LANES = 128
MESH = pl.DeviceIdType.MESH


def tables(rows, cols):
    length = rows * cols
    shifted = np.arange(rows, dtype=np.float64) + 0.25
    first = 2.0 * np.pi * np.outer(shifted, np.arange(rows)) / rows
    turn = 2.0 * np.pi * np.outer(shifted, np.arange(cols)) / length
    second = 2.0 * np.pi * (np.outer(np.arange(cols), np.arange(cols)) % cols) / cols
    return tuple(
        table.astype(np.float32)
        for table in (
            np.concatenate([np.cos(first), -np.sin(first)], 0),
            np.stack([np.cos(turn), -np.sin(turn)]),
            np.stack([np.cos(second), np.sin(second)]),
            np.concatenate([np.cos(first).T, -np.sin(first).T], 1) / length,
        )
    )


def dot(left, right):
    return jnp.dot(left, right, preferred_element_type=F32)


def halves(value):
    high = value.astype(BF16)
    return high, (value - high.astype(F32)).astype(BF16)


def forward(block, t_first, t_turn, t_forward):
    rows, cols = block.shape
    mixed = dot(t_first[0], block) + dot(t_first[1], block)
    real, imag = mixed[:rows], mixed[rows:]
    turn_re, turn_im = t_turn[0], t_turn[1]
    turned = jnp.concatenate(
        [real * turn_re - imag * turn_im, real * turn_im + imag * turn_re], axis=1
    )
    high, low = halves(turned)
    spec = dot(high, t_forward[0]) + dot(low, t_forward[0]) + dot(high, t_forward[1])
    return spec[:, :cols], spec[:, cols:]


def inverse(real, imag, t_turn, t_back, t_last):
    cols = real.shape[1]
    high, low = halves(jnp.concatenate([real, imag], axis=1))
    mixed = dot(high, t_back[0]) + dot(low, t_back[0]) + dot(high, t_back[1])
    real, imag = mixed[:, :cols], mixed[:, cols:]
    turn_re, turn_im = t_turn[0], t_turn[1]
    high, low = halves(
        jnp.concatenate([real * turn_re + imag * turn_im, imag * turn_re - real * turn_im], axis=0)
    )
    return dot(t_last[0], high) + dot(t_last[0], low) + dot(t_last[1], high)


def layer(
    n_dp,
    n_ctx,
    x_hbm,
    g_hbm,
    master_hbm,
    one_hbm,
    two_hbm,
    n_hbm,
    first_hbm,
    turn_hbm,
    second_hbm,
    last_hbm,
    master_out,
    one_out,
    two_out,
    out_recv,
    raw,
    mixed,
    block_send,
    block_recv,
    w_first,
    t_turn,
    w_second,
    w_last,
    t_first,
    t_forward,
    t_back,
    t_last,
    state_in,
    state,
    state_out,
    spec,
    partial,
    grad_send,
    grad_recv,
    filt,
    out_send,
    local_sem,
    store_sem,
    block_ssem,
    block_rsem,
    grad_ssem,
    grad_rsem,
    filt_ssem,
    filt_rsem,
    out_ssem,
    out_rsem,
):
    me_dp = lax.axis_index("dp")
    me = lax.axis_index("ctx")
    channels = raw.shape[1]
    owned = block_recv.shape[1]
    rows_block, cols = block_send.shape[2:]
    rows = n_ctx * rows_block
    rows_own = filt.shape[2]

    barrier = pltpu.get_barrier_semaphore()

    def greet_ctx(i, carry):
        peer = lax.rem(me + i, n_ctx)
        pl.semaphore_signal(barrier, inc=1, device_id={"ctx": peer}, device_id_type=MESH)
        return carry

    def greet_dp(i, carry):
        peer = lax.rem(me_dp + i, n_dp)
        pl.semaphore_signal(barrier, inc=1, device_id={"dp": peer}, device_id_type=MESH)
        return carry

    lax.fori_loop(1, n_ctx, greet_ctx, 0)
    lax.fori_loop(1, n_dp, greet_dp, 0)

    loads = []
    for source, target in (
        (x_hbm.at[0], raw.at[0]),
        (g_hbm.at[0], raw.at[1]),
        (first_hbm, w_first),
        (turn_hbm, t_turn),
        (second_hbm, w_second),
        (last_hbm, w_last),
        (n_hbm.at[0], raw.at[2]),
        (master_hbm, state_in.at[0]),
        (one_hbm, state_in.at[1]),
        (two_hbm, state_in.at[2]),
    ):
        copy = pltpu.make_async_copy(source, target, local_sem.at[len(loads)])
        copy.start()
        loads.append(copy)

    def regroup(which):
        for i in range(rows_block):
            part = raw[which, :, i * cols : (i + 1) * cols].astype(F32)
            for lane in range(cols // LANES):
                mixed[lane, i * channels : (i + 1) * channels, :] = part[
                    :, lane * LANES : (lane + 1) * LANES
                ]
        for c in range(channels):
            for lane in range(cols // LANES):
                block_send[which, c, :, lane * LANES : (lane + 1) * LANES] = mixed[
                    lane, pl.ds(c, rows_block, stride=channels), :
                ].astype(BF16)

    def send_block(which, ch):
        def one(i, carry):
            peer = lax.rem(me + i, n_ctx)
            pltpu.make_async_remote_copy(
                src_ref=block_send.at[which, peer * owned + ch],
                dst_ref=block_recv.at[which, ch, me],
                send_sem=block_ssem.at[which, ch],
                recv_sem=block_rsem.at[which, ch],
                device_id={"ctx": peer},
                device_id_type=MESH,
            ).start()
            return carry

        lax.fori_loop(1, n_ctx, one, 0)
        block_recv[which, ch, me] = block_send[which, me * owned + ch]

    def wait_bytes(ref, count, sem):
        part = ref.at[pl.ds(0, count)]
        pltpu.make_async_copy(part, part, sem).wait()

    def wait_block(which, ch):
        wait_bytes(block_recv.at[which, ch], n_ctx - 1, block_rsem.at[which, ch])
        return block_recv[which, ch].reshape(rows, cols)

    def spectrum(block):
        return forward(block, t_first, t_turn, t_forward)

    loads[0].wait()
    regroup(0)
    pl.semaphore_wait(barrier, n_ctx + n_dp - 2)
    send_block(0, 0)
    loads[1].wait()
    regroup(1)
    send_block(1, 0)
    for ch in range(1, owned):
        send_block(0, ch)
        send_block(1, ch)
    for copy in loads[2:]:
        copy.wait()
    t_first[0], t_first[1] = halves(w_first[...])
    t_last[0], t_last[1] = halves(w_last[...])
    low_cols, high_cols = slice(0, cols), slice(cols, 2 * cols)
    for part, (cosine, sine) in enumerate(zip(halves(w_second[0]), halves(w_second[1]))):
        for table, upper, lower in ((t_forward, -sine, sine), (t_back, sine, -sine)):
            table[part, low_cols, low_cols] = cosine
            table[part, low_cols, high_cols] = upper
            table[part, high_cols, low_cols] = lower
            table[part, high_cols, high_cols] = cosine
    regroup(2)

    def fold_row(i, carry):
        span = pl.ds(pl.multiple_of(i * cols, LANES), cols)
        for which in range(3):
            for ch in range(owned):
                state[which, ch, pl.ds(i, 1), :] = state_in[which, ch : ch + 1, span]
        return carry

    lax.fori_loop(0, rows_own, fold_row, 0, unroll=4)

    def keep(values):
        spec[0], spec[1] = values

    def gradient(ch):
        g_block = wait_block(1, ch)
        if ch == owned - 1:
            for later in range(owned):
                send_block(2, later)
        g_re, g_im = spectrum(g_block)
        x_re, x_im = spec[0], spec[1]
        total = inverse(
            x_re * g_re + x_im * g_im, x_re * g_im - x_im * g_re, t_turn, t_back, t_last
        ).reshape(n_dp, rows_own, cols)
        partial[ch] = total
        grad_send[ch] = total.astype(BF16)

        def one(i, carry):
            peer = lax.rem(me_dp + i, n_dp)
            pltpu.make_async_remote_copy(
                src_ref=grad_send.at[ch, peer],
                dst_ref=grad_recv.at[ch, i - 1],
                send_sem=grad_ssem.at[ch],
                recv_sem=grad_rsem.at[ch],
                device_id={"dp": peer},
                device_id_type=MESH,
            ).start()
            return carry

        lax.fori_loop(1, n_dp, one, 0)

    def update(ch):
        wait_bytes(grad_recv.at[ch], n_dp - 1, grad_rsem.at[ch])
        grad = partial[ch, me_dp]
        for i in range(n_dp - 1):
            grad = grad + grad_recv[ch, i].astype(F32)
        master = state[0, ch]
        new_one = 0.9 * state[1, ch] + 0.1 * grad
        new_two = 0.999 * state[2, ch] + 0.001 * grad * grad
        first_hat = new_one / (1.0 - 0.9**10)
        second_hat = new_two / (1.0 - 0.999**10)
        new_master = master - 0.01 * (first_hat / (jnp.sqrt(second_hat) + 1e-08) + 0.1 * master)
        filt[ch, me_dp] = new_master.astype(BF16)

        def one(i, carry):
            peer = lax.rem(me_dp + i, n_dp)
            pltpu.make_async_remote_copy(
                src_ref=filt.at[ch, me_dp],
                dst_ref=filt.at[ch, me_dp],
                send_sem=filt_ssem.at[ch],
                recv_sem=filt_rsem.at[ch],
                device_id={"dp": peer},
                device_id_type=MESH,
            ).start()
            return carry

        lax.fori_loop(1, n_dp, one, 0)
        for which, value in enumerate((new_master, new_one, new_two)):
            state[which, ch] = value

        def flat_row(i, carry):
            span = pl.ds(pl.multiple_of(i * cols, LANES), cols)
            for which in range(3):
                state_out[which, ch : ch + 1, span] = state[which, ch, pl.ds(i, 1), :]
            return carry

        lax.fori_loop(0, rows_own, flat_row, 0, unroll=8)

    def product(ch):
        wait_bytes(filt.at[ch], n_dp - 1, filt_rsem.at[ch])
        f_re, f_im = spectrum(filt[ch].reshape(rows, cols))
        x_re, x_im = spec[0], spec[1]
        keep((x_re * f_re - x_im * f_im, x_re * f_im + x_im * f_re))

    def finish(ch):
        result = inverse(spec[0], spec[1], t_turn, t_back, t_last)
        out_send[ch] = result.astype(BF16).reshape(n_ctx, rows_block, cols)

        def one(i, carry):
            peer = lax.rem(me + i, n_ctx)
            pltpu.make_async_remote_copy(
                src_ref=out_send.at[ch, peer],
                dst_ref=out_recv.at[me * owned + ch],
                send_sem=out_ssem.at[ch],
                recv_sem=out_rsem.at[ch],
                device_id={"ctx": peer},
                device_id_type=MESH,
            ).start()
            return carry

        lax.fori_loop(1, n_ctx, one, 0)
        copy = pltpu.make_async_copy(
            out_send.at[ch, me], out_recv.at[me * owned + ch], local_sem.at[ch]
        )
        copy.start()
        stores.append(copy)

    stores = []
    for ch in range(owned):
        keep(spectrum(wait_block(0, ch)))
        if ch:
            update(ch - 1)
        gradient(ch)
    final = owned - 1
    for ch in range(final):
        keep(spectrum(wait_block(2, ch)))
        product(ch)
        if ch == final - 1:
            update(final)
        finish(ch)
    if not final:
        update(final)
    keep(spectrum(wait_block(2, final)))
    product(final)
    for which, target in enumerate((master_out, one_out, two_out)):
        copy = pltpu.make_async_copy(state_out.at[which], target, store_sem.at[which])
        copy.start()
        stores.append(copy)
    finish(final)
    for ch in range(owned):
        for which in range(3):
            wait_bytes(block_send.at[which], n_ctx - 1, block_ssem.at[which, ch])
        wait_bytes(grad_send.at[ch], n_dp - 1, grad_ssem.at[ch])
        wait_bytes(filt.at[ch], n_dp - 1, filt_ssem.at[ch])
        wait_bytes(out_send.at[ch], n_ctx - 1, out_ssem.at[ch])
    for ch in range(owned):
        wait_bytes(out_recv, n_ctx - 1, out_rsem.at[ch])
    for copy in stores:
        copy.wait()


def settle(
    master, one, two, blocks, master_out, one_out, two_out, next_out, held, block, mixed, flat, sems
):
    channels, rows_block, cols = block.shape
    load = pltpu.make_async_copy(blocks, block, sems.at[0])
    load.start()
    loads = [
        pltpu.make_async_copy(source, held.at[i], sems.at[1 + i])
        for i, source in enumerate((master, one, two))
    ]
    stores = [
        pltpu.make_async_copy(held.at[i], target, sems.at[4 + i])
        for i, target in enumerate((master_out, one_out, two_out))
    ]
    for copy in loads:
        copy.start()
    load.wait()
    for c in range(channels):
        part = block[c].astype(F32)
        for lane in range(cols // LANES):
            mixed[lane, c * rows_block : (c + 1) * rows_block, :] = part[
                :, lane * LANES : (lane + 1) * LANES
            ]
    for before, after in zip(loads, stores):
        before.wait()
        after.start()
    for i in range(rows_block):
        for lane in range(cols // LANES):
            start = i * cols + lane * LANES
            flat[:, start : start + LANES] = mixed[
                lane, pl.ds(i, channels, stride=rows_block), :
            ].astype(BF16)
    store = pltpu.make_async_copy(flat, next_out.at[0], sems.at[7])
    store.start()
    for copy in stores:
        copy.wait()
    store.wait()


def local(n_dp, n_ctx, inputs, out_grad, master, moment_one, moment_two, next_inputs):
    channels, span = inputs.shape[1:]
    owned, taps_own = master.shape
    length = n_ctx * span
    cols = min(256, span // 16)
    rows = length // cols
    rows_block, rows_own = span // cols, taps_own // cols
    table_list = tables(rows, cols)
    dma = pltpu.SemaphoreType.DMA
    vmem = pltpu.VMEM
    anywhere = pl.BlockSpec(memory_space=pltpu.HBM)
    macs = 12 * owned * length * (rows + 2 * cols) * 3
    results = pl.pallas_call(
        functools.partial(layer, n_dp, n_ctx),
        name="layer",
        out_shape=(
            jax.ShapeDtypeStruct(master.shape, F32),
            jax.ShapeDtypeStruct(master.shape, F32),
            jax.ShapeDtypeStruct(master.shape, F32),
            jax.ShapeDtypeStruct((channels, rows_block, cols), BF16),
        ),
        in_specs=[anywhere] * 10,
        out_specs=[anywhere] * 4,
        scratch_shapes=[
            vmem((3, channels, span), BF16),
            vmem((cols // LANES, channels * rows_block, LANES), F32),
            vmem((3, channels, rows_block, cols), BF16),
            vmem((3, owned, n_ctx, rows_block, cols), BF16),
            *[vmem(table.shape, F32) for table in table_list],
            vmem((2, 2 * rows, rows), BF16),
            vmem((2, 2 * cols, 2 * cols), BF16),
            vmem((2, 2 * cols, 2 * cols), BF16),
            vmem((2, rows, 2 * rows), BF16),
            vmem((3, owned, taps_own), F32),
            vmem((3, owned, rows_own, cols), F32),
            vmem((3, owned, taps_own), F32),
            vmem((2, rows, cols), F32),
            vmem((owned, n_dp, rows_own, cols), F32),
            vmem((owned, n_dp, rows_own, cols), BF16),
            vmem((owned, n_dp - 1, rows_own, cols), BF16),
            vmem((owned, n_dp, rows_own, cols), BF16),
            vmem((owned, n_ctx, rows_block, cols), BF16),
            dma((10,)),
            dma((3,)),
            dma((3, owned)),
            dma((3, owned)),
            dma((owned,)),
            dma((owned,)),
            dma((owned,)),
            dma((owned,)),
            dma((owned,)),
            dma((owned,)),
        ],
        compiler_params=pltpu.CompilerParams(
            collective_id=0, has_side_effects=True, vmem_limit_bytes=56 * 1024 * 1024
        ),
        cost_estimate=pl.CostEstimate(
            flops=2 * macs, bytes_accessed=8 * 1024 * 1024, transcendentals=0
        ),
    )(inputs, out_grad, master, moment_one, moment_two, next_inputs, *table_list)
    return pl.pallas_call(
        settle,
        name="settle",
        out_shape=(
            jax.ShapeDtypeStruct(master.shape, F32),
            jax.ShapeDtypeStruct(master.shape, F32),
            jax.ShapeDtypeStruct(master.shape, F32),
            jax.ShapeDtypeStruct(inputs.shape, BF16),
        ),
        in_specs=[anywhere] * 4,
        out_specs=[anywhere] * 4,
        scratch_shapes=[
            vmem((3, owned, taps_own), F32),
            vmem((channels, rows_block, cols), BF16),
            vmem((cols // LANES, channels * rows_block, LANES), F32),
            vmem((channels, span), BF16),
            dma((8,)),
        ],
        compiler_params=pltpu.CompilerParams(vmem_limit_bytes=56 * 1024 * 1024),
    )(*results)


def solution(mesh):
    return jax.shard_map(
        functools.partial(local, mesh.shape["dp"], mesh.shape["ctx"]),
        mesh=mesh,
        in_specs=(
            P("dp", None, "ctx"),
            P("dp", None, "ctx"),
            P("ctx", "dp"),
            P("ctx", "dp"),
            P("ctx", "dp"),
            P("dp", None, "ctx"),
        ),
        out_specs=(P("ctx", "dp"), P("ctx", "dp"), P("ctx", "dp"), P("dp", None, "ctx")),
        check_vma=False,
    )
```

```python
import functools

import jax
import jax.numpy as jnp
import numpy as np
from jax import lax
from jax.experimental import pallas as pl
from jax.experimental.pallas import tpu as pltpu
from jax.sharding import PartitionSpec as P

F32 = jnp.float32
BF16 = jnp.bfloat16
LANES = 128
MESH = pl.DeviceIdType.MESH


def tables(rows, cols):
    length = rows * cols
    shifted = np.arange(rows, dtype=np.float64) + 0.25
    first = 2.0 * np.pi * np.outer(shifted, np.arange(rows)) / rows
    turn = 2.0 * np.pi * np.outer(shifted, np.arange(cols)) / length
    second = 2.0 * np.pi * (np.outer(np.arange(cols), np.arange(cols)) % cols) / cols
    return tuple(
        table.astype(np.float32)
        for table in (
            np.concatenate([np.cos(first), -np.sin(first)], 0),
            np.stack([np.cos(turn), -np.sin(turn)]),
            np.stack([np.cos(second), np.sin(second)]),
            np.concatenate([np.cos(first).T, -np.sin(first).T], 1) / length,
        )
    )


def dot(left, right):
    return jnp.dot(left, right, preferred_element_type=F32)


def halves(value):
    high = value.astype(BF16)
    return high, (value - high.astype(F32)).astype(BF16)


def forward(block, t_first, t_turn, t_forward):
    rows, cols = block.shape
    mixed = dot(t_first[0], block) + dot(t_first[1], block)
    real, imag = mixed[:rows], mixed[rows:]
    turn_re, turn_im = t_turn[0], t_turn[1]
    turned = jnp.concatenate(
        [real * turn_re - imag * turn_im, real * turn_im + imag * turn_re], axis=1
    )
    high, low = halves(turned)
    spec = dot(high, t_forward[0]) + dot(low, t_forward[0]) + dot(high, t_forward[1])
    return spec[:, :cols], spec[:, cols:]


def inverse(real, imag, t_turn, t_back, t_last):
    cols = real.shape[1]
    high, low = halves(jnp.concatenate([real, imag], axis=1))
    mixed = dot(high, t_back[0]) + dot(low, t_back[0]) + dot(high, t_back[1])
    real, imag = mixed[:, :cols], mixed[:, cols:]
    turn_re, turn_im = t_turn[0], t_turn[1]
    high, low = halves(
        jnp.concatenate([real * turn_re + imag * turn_im, imag * turn_re - real * turn_im], axis=0)
    )
    return dot(t_last[0], high) + dot(t_last[0], low) + dot(t_last[1], high)


def layer(
    n_dp,
    n_ctx,
    x_hbm,
    g_hbm,
    master_hbm,
    one_hbm,
    two_hbm,
    n_hbm,
    first_hbm,
    turn_hbm,
    second_hbm,
    last_hbm,
    master_out,
    one_out,
    two_out,
    out_recv,
    raw,
    mixed,
    block_send,
    block_recv,
    w_first,
    t_turn,
    w_second,
    w_last,
    t_first,
    t_forward,
    t_back,
    t_last,
    state_in,
    state,
    state_out,
    spec,
    partial,
    grad_send,
    grad_recv,
    filt,
    out_send,
    local_sem,
    store_sem,
    block_ssem,
    block_rsem,
    grad_ssem,
    grad_rsem,
    filt_ssem,
    filt_rsem,
    out_ssem,
    out_rsem,
):
    me_dp = lax.axis_index("dp")
    me = lax.axis_index("ctx")
    channels = raw.shape[1]
    owned = block_recv.shape[1]
    rows_block, cols = block_send.shape[2:]
    rows = n_ctx * rows_block
    rows_own = filt.shape[2]

    barrier = pltpu.get_barrier_semaphore()

    def greet_ctx(i, carry):
        peer = lax.rem(me + i, n_ctx)
        pl.semaphore_signal(barrier, inc=1, device_id={"ctx": peer}, device_id_type=MESH)
        return carry

    def greet_dp(i, carry):
        peer = lax.rem(me_dp + i, n_dp)
        pl.semaphore_signal(barrier, inc=1, device_id={"dp": peer}, device_id_type=MESH)
        return carry

    lax.fori_loop(1, n_ctx, greet_ctx, 0)
    lax.fori_loop(1, n_dp, greet_dp, 0)

    loads = []
    for source, target in (
        (x_hbm.at[0], raw.at[0]),
        (g_hbm.at[0], raw.at[1]),
        (first_hbm, w_first),
        (turn_hbm, t_turn),
        (second_hbm, w_second),
        (last_hbm, w_last),
        (n_hbm.at[0], raw.at[2]),
        (master_hbm, state_in.at[0]),
        (one_hbm, state_in.at[1]),
        (two_hbm, state_in.at[2]),
    ):
        copy = pltpu.make_async_copy(source, target, local_sem.at[len(loads)])
        copy.start()
        loads.append(copy)

    def regroup(which):
        for i in range(rows_block):
            part = raw[which, :, i * cols : (i + 1) * cols].astype(F32)
            for lane in range(cols // LANES):
                mixed[lane, i * channels : (i + 1) * channels, :] = part[
                    :, lane * LANES : (lane + 1) * LANES
                ]
        for c in range(channels):
            for lane in range(cols // LANES):
                block_send[which, c, :, lane * LANES : (lane + 1) * LANES] = mixed[
                    lane, pl.ds(c, rows_block, stride=channels), :
                ].astype(BF16)

    def send_block(which, ch):
        def one(i, carry):
            peer = lax.rem(me + i, n_ctx)
            pltpu.make_async_remote_copy(
                src_ref=block_send.at[which, peer * owned + ch],
                dst_ref=block_recv.at[which, ch, me],
                send_sem=block_ssem.at[which, ch],
                recv_sem=block_rsem.at[which, ch],
                device_id={"ctx": peer},
                device_id_type=MESH,
            ).start()
            return carry

        lax.fori_loop(1, n_ctx, one, 0)
        block_recv[which, ch, me] = block_send[which, me * owned + ch]

    def wait_bytes(ref, count, sem):
        part = ref.at[pl.ds(0, count)]
        pltpu.make_async_copy(part, part, sem).wait()

    def wait_block(which, ch):
        wait_bytes(block_recv.at[which, ch], n_ctx - 1, block_rsem.at[which, ch])
        return block_recv[which, ch].reshape(rows, cols)

    def spectrum(block):
        return forward(block, t_first, t_turn, t_forward)

    loads[0].wait()
    regroup(0)
    pl.semaphore_wait(barrier, n_ctx + n_dp - 2)
    send_block(0, 0)
    loads[1].wait()
    regroup(1)
    send_block(1, 0)
    for copy in loads[2:]:
        copy.wait()
    t_first[0], t_first[1] = halves(w_first[...])
    t_last[0], t_last[1] = halves(w_last[...])
    low_cols, high_cols = slice(0, cols), slice(cols, 2 * cols)
    for part, (cosine, sine) in enumerate(zip(halves(w_second[0]), halves(w_second[1]))):
        for table, upper, lower in ((t_forward, -sine, sine), (t_back, sine, -sine)):
            table[part, low_cols, low_cols] = cosine
            table[part, low_cols, high_cols] = upper
            table[part, high_cols, low_cols] = lower
            table[part, high_cols, high_cols] = cosine
    regroup(2)

    def fold_row(i, carry):
        span = pl.ds(pl.multiple_of(i * cols, LANES), cols)
        for which in range(3):
            for ch in range(owned):
                state[which, ch, pl.ds(i, 1), :] = state_in[which, ch : ch + 1, span]
        return carry

    lax.fori_loop(0, rows_own, fold_row, 0, unroll=4)

    def keep(values):
        spec[0], spec[1] = values

    def gradient(ch):
        g_block = wait_block(1, ch)
        send_block(*((1, ch + 1) if ch + 1 < owned else (2, 0)))
        g_re, g_im = spectrum(g_block)
        x_re, x_im = spec[0], spec[1]
        total = inverse(
            x_re * g_re + x_im * g_im, x_re * g_im - x_im * g_re, t_turn, t_back, t_last
        ).reshape(n_dp, rows_own, cols)
        partial[ch] = total
        grad_send[ch] = total.astype(BF16)

        def one(i, carry):
            peer = lax.rem(me_dp + i, n_dp)
            pltpu.make_async_remote_copy(
                src_ref=grad_send.at[ch, peer],
                dst_ref=grad_recv.at[ch, i - 1],
                send_sem=grad_ssem.at[ch],
                recv_sem=grad_rsem.at[ch],
                device_id={"dp": peer},
                device_id_type=MESH,
            ).start()
            return carry

        lax.fori_loop(1, n_dp, one, 0)

    def update(ch):
        wait_bytes(grad_recv.at[ch], n_dp - 1, grad_rsem.at[ch])
        grad = partial[ch, me_dp]
        for i in range(n_dp - 1):
            grad = grad + grad_recv[ch, i].astype(F32)
        master = state[0, ch]
        new_one = 0.9 * state[1, ch] + 0.1 * grad
        new_two = 0.999 * state[2, ch] + 0.001 * grad * grad
        first_hat = new_one / (1.0 - 0.9**10)
        second_hat = new_two / (1.0 - 0.999**10)
        new_master = master - 0.01 * (first_hat / (jnp.sqrt(second_hat) + 1e-08) + 0.1 * master)
        filt[ch, me_dp] = new_master.astype(BF16)

        def one(i, carry):
            peer = lax.rem(me_dp + i, n_dp)
            pltpu.make_async_remote_copy(
                src_ref=filt.at[ch, me_dp],
                dst_ref=filt.at[ch, me_dp],
                send_sem=filt_ssem.at[ch],
                recv_sem=filt_rsem.at[ch],
                device_id={"dp": peer},
                device_id_type=MESH,
            ).start()
            return carry

        lax.fori_loop(1, n_dp, one, 0)
        for which, value in enumerate((new_master, new_one, new_two)):
            state[which, ch] = value

        def flat_row(i, carry):
            span = pl.ds(pl.multiple_of(i * cols, LANES), cols)
            for which in range(3):
                state_out[which, ch : ch + 1, span] = state[which, ch, pl.ds(i, 1), :]
            return carry

        lax.fori_loop(0, rows_own, flat_row, 0, unroll=8)

    def product(ch):
        wait_bytes(filt.at[ch], n_dp - 1, filt_rsem.at[ch])
        f_re, f_im = spectrum(filt[ch].reshape(rows, cols))
        x_re, x_im = spec[0], spec[1]
        keep((x_re * f_re - x_im * f_im, x_re * f_im + x_im * f_re))

    def finish(ch):
        result = inverse(spec[0], spec[1], t_turn, t_back, t_last)
        out_send[ch] = result.astype(BF16).reshape(n_ctx, rows_block, cols)

        def one(i, carry):
            peer = lax.rem(me + i, n_ctx)
            pltpu.make_async_remote_copy(
                src_ref=out_send.at[ch, peer],
                dst_ref=out_recv.at[me * owned + ch],
                send_sem=out_ssem.at[ch],
                recv_sem=out_rsem.at[ch],
                device_id={"ctx": peer},
                device_id_type=MESH,
            ).start()
            return carry

        lax.fori_loop(1, n_ctx, one, 0)
        copy = pltpu.make_async_copy(
            out_send.at[ch, me], out_recv.at[me * owned + ch], local_sem.at[ch]
        )
        copy.start()
        stores.append(copy)

    stores = []
    for ch in range(owned):
        x_block = wait_block(0, ch)
        if ch + 1 < owned:
            send_block(0, ch + 1)
        keep(spectrum(x_block))
        if ch:
            update(ch - 1)
        gradient(ch)
    final = owned - 1
    for ch in range(final):
        send_block(2, ch + 1)
        keep(spectrum(wait_block(2, ch)))
        product(ch)
        if ch == final - 1:
            update(final)
        finish(ch)
    if not final:
        update(final)
    keep(spectrum(wait_block(2, final)))
    product(final)
    for which, target in enumerate((master_out, one_out, two_out)):
        copy = pltpu.make_async_copy(state_out.at[which], target, store_sem.at[which])
        copy.start()
        stores.append(copy)
    finish(final)
    for ch in range(owned):
        for which in range(3):
            wait_bytes(block_send.at[which], n_ctx - 1, block_ssem.at[which, ch])
        wait_bytes(grad_send.at[ch], n_dp - 1, grad_ssem.at[ch])
        wait_bytes(filt.at[ch], n_dp - 1, filt_ssem.at[ch])
        wait_bytes(out_send.at[ch], n_ctx - 1, out_ssem.at[ch])
    for ch in range(owned):
        wait_bytes(out_recv, n_ctx - 1, out_rsem.at[ch])
    for copy in stores:
        copy.wait()


def settle(
    master, one, two, blocks, master_out, one_out, two_out, next_out, held, block, mixed, flat, sems
):
    channels, rows_block, cols = block.shape
    load = pltpu.make_async_copy(blocks, block, sems.at[0])
    load.start()
    loads = [
        pltpu.make_async_copy(source, held.at[i], sems.at[1 + i])
        for i, source in enumerate((master, one, two))
    ]
    stores = [
        pltpu.make_async_copy(held.at[i], target, sems.at[4 + i])
        for i, target in enumerate((master_out, one_out, two_out))
    ]
    for copy in loads:
        copy.start()
    load.wait()
    for c in range(channels):
        part = block[c].astype(F32)
        for lane in range(cols // LANES):
            mixed[lane, c * rows_block : (c + 1) * rows_block, :] = part[
                :, lane * LANES : (lane + 1) * LANES
            ]
    for before, after in zip(loads, stores):
        before.wait()
        after.start()
    for i in range(rows_block):
        for lane in range(cols // LANES):
            start = i * cols + lane * LANES
            flat[:, start : start + LANES] = mixed[
                lane, pl.ds(i, channels, stride=rows_block), :
            ].astype(BF16)
    store = pltpu.make_async_copy(flat, next_out.at[0], sems.at[7])
    store.start()
    for copy in stores:
        copy.wait()
    store.wait()


def local(n_dp, n_ctx, inputs, out_grad, master, moment_one, moment_two, next_inputs):
    channels, span = inputs.shape[1:]
    owned, taps_own = master.shape
    length = n_ctx * span
    cols = min(256, span // 16)
    rows = length // cols
    rows_block, rows_own = span // cols, taps_own // cols
    table_list = tables(rows, cols)
    dma = pltpu.SemaphoreType.DMA
    vmem = pltpu.VMEM
    anywhere = pl.BlockSpec(memory_space=pltpu.HBM)
    macs = 12 * owned * length * (rows + 2 * cols) * 3
    results = pl.pallas_call(
        functools.partial(layer, n_dp, n_ctx),
        name="layer",
        out_shape=(
            jax.ShapeDtypeStruct(master.shape, F32),
            jax.ShapeDtypeStruct(master.shape, F32),
            jax.ShapeDtypeStruct(master.shape, F32),
            jax.ShapeDtypeStruct((channels, rows_block, cols), BF16),
        ),
        in_specs=[anywhere] * 10,
        out_specs=[anywhere] * 4,
        scratch_shapes=[
            vmem((3, channels, span), BF16),
            vmem((cols // LANES, channels * rows_block, LANES), F32),
            vmem((3, channels, rows_block, cols), BF16),
            vmem((3, owned, n_ctx, rows_block, cols), BF16),
            *[vmem(table.shape, F32) for table in table_list],
            vmem((2, 2 * rows, rows), BF16),
            vmem((2, 2 * cols, 2 * cols), BF16),
            vmem((2, 2 * cols, 2 * cols), BF16),
            vmem((2, rows, 2 * rows), BF16),
            vmem((3, owned, taps_own), F32),
            vmem((3, owned, rows_own, cols), F32),
            vmem((3, owned, taps_own), F32),
            vmem((2, rows, cols), F32),
            vmem((owned, n_dp, rows_own, cols), F32),
            vmem((owned, n_dp, rows_own, cols), BF16),
            vmem((owned, n_dp - 1, rows_own, cols), BF16),
            vmem((owned, n_dp, rows_own, cols), BF16),
            vmem((owned, n_ctx, rows_block, cols), BF16),
            dma((10,)),
            dma((3,)),
            dma((3, owned)),
            dma((3, owned)),
            dma((owned,)),
            dma((owned,)),
            dma((owned,)),
            dma((owned,)),
            dma((owned,)),
            dma((owned,)),
        ],
        compiler_params=pltpu.CompilerParams(
            collective_id=0, has_side_effects=True, vmem_limit_bytes=56 * 1024 * 1024
        ),
        cost_estimate=pl.CostEstimate(
            flops=2 * macs, bytes_accessed=8 * 1024 * 1024, transcendentals=0
        ),
    )(inputs, out_grad, master, moment_one, moment_two, next_inputs, *table_list)
    return pl.pallas_call(
        settle,
        name="settle",
        out_shape=(
            jax.ShapeDtypeStruct(master.shape, F32),
            jax.ShapeDtypeStruct(master.shape, F32),
            jax.ShapeDtypeStruct(master.shape, F32),
            jax.ShapeDtypeStruct(inputs.shape, BF16),
        ),
        in_specs=[anywhere] * 4,
        out_specs=[anywhere] * 4,
        scratch_shapes=[
            vmem((3, owned, taps_own), F32),
            vmem((channels, rows_block, cols), BF16),
            vmem((cols // LANES, channels * rows_block, LANES), F32),
            vmem((channels, span), BF16),
            dma((8,)),
        ],
        compiler_params=pltpu.CompilerParams(vmem_limit_bytes=56 * 1024 * 1024),
    )(*results)


def solution(mesh):
    return jax.shard_map(
        functools.partial(local, mesh.shape["dp"], mesh.shape["ctx"]),
        mesh=mesh,
        in_specs=(
            P("dp", None, "ctx"),
            P("dp", None, "ctx"),
            P("ctx", "dp"),
            P("ctx", "dp"),
            P("ctx", "dp"),
            P("dp", None, "ctx"),
        ),
        out_specs=(P("ctx", "dp"), P("ctx", "dp"), P("ctx", "dp"), P("dp", None, "ctx")),
        check_vma=False,
    )
```

```python
import functools

import jax
import jax.numpy as jnp
import numpy as np
from jax import lax
from jax.experimental import pallas as pl
from jax.experimental.pallas import tpu as pltpu
from jax.sharding import PartitionSpec as P

F32 = jnp.float32
BF16 = jnp.bfloat16
LANES = 128
MESH = pl.DeviceIdType.MESH


def tables(rows, cols):
    length = rows * cols
    shifted = np.arange(rows, dtype=np.float64) + 0.25
    first = 2.0 * np.pi * np.outer(shifted, np.arange(rows)) / rows
    turn = 2.0 * np.pi * np.outer(shifted, np.arange(cols)) / length
    second = 2.0 * np.pi * (np.outer(np.arange(cols), np.arange(cols)) % cols) / cols
    return tuple(
        table.astype(np.float32)
        for table in (
            np.concatenate([np.cos(first), -np.sin(first)], 0),
            np.stack([np.cos(turn), -np.sin(turn)]),
            np.stack([np.cos(second), np.sin(second)]),
            np.concatenate([np.cos(first).T, -np.sin(first).T], 1) / length,
        )
    )


def dot(left, right):
    return jnp.dot(left, right, preferred_element_type=F32)


def halves(value):
    high = value.astype(BF16)
    return high, (value - high.astype(F32)).astype(BF16)


def thrice(value, table):
    rows = value.shape[0]
    high, low = halves(value)
    both = dot(jnp.concatenate([high, low], axis=0), table[0])
    return both[:rows] + (both[rows:] + dot(high, table[1]))


def forward(block, t_first, t_turn, t_forward):
    rows, cols = block.shape
    mixed = dot(t_first[...], block)
    real = mixed[:rows] + mixed[2 * rows : 3 * rows]
    imag = mixed[rows : 2 * rows] + mixed[3 * rows :]
    turn_re, turn_im = t_turn[0], t_turn[1]
    turned = jnp.concatenate(
        [real * turn_re - imag * turn_im, real * turn_im + imag * turn_re], axis=1
    )
    spec = thrice(turned, t_forward)
    return spec[:, :cols], spec[:, cols:]


def inverse(real, imag, t_turn, t_back, t_last):
    cols = real.shape[1]
    rows = real.shape[0]
    mixed = thrice(jnp.concatenate([real, imag], axis=1), t_back)
    real, imag = mixed[:, :cols], mixed[:, cols:]
    turn_re, turn_im = t_turn[0], t_turn[1]
    high, low = halves(
        jnp.concatenate([real * turn_re + imag * turn_im, imag * turn_re - real * turn_im], axis=0)
    )
    both = dot(t_last[...], high)
    return both[:rows] + (both[rows:] + dot(t_last[:rows], low))


def layer(
    n_dp,
    n_ctx,
    x_hbm,
    g_hbm,
    master_hbm,
    one_hbm,
    two_hbm,
    n_hbm,
    first_hbm,
    turn_hbm,
    second_hbm,
    last_hbm,
    master_out,
    one_out,
    two_out,
    out_recv,
    raw,
    mixed,
    block_send,
    block_recv,
    w_first,
    t_turn,
    w_second,
    w_last,
    t_first,
    t_forward,
    t_back,
    t_last,
    state_in,
    state,
    state_out,
    spec,
    partial,
    grad_send,
    grad_recv,
    filt,
    out_send,
    local_sem,
    store_sem,
    block_ssem,
    block_rsem,
    grad_ssem,
    grad_rsem,
    filt_ssem,
    filt_rsem,
    out_ssem,
    out_rsem,
):
    me_dp = lax.axis_index("dp")
    me = lax.axis_index("ctx")
    channels = raw.shape[1]
    owned = block_recv.shape[1]
    rows_block, cols = block_send.shape[2:]
    rows = n_ctx * rows_block
    rows_own = filt.shape[2]

    barrier = pltpu.get_barrier_semaphore()

    def greet_ctx(i, carry):
        peer = lax.rem(me + i, n_ctx)
        pl.semaphore_signal(barrier, inc=1, device_id={"ctx": peer}, device_id_type=MESH)
        return carry

    def greet_dp(i, carry):
        peer = lax.rem(me_dp + i, n_dp)
        pl.semaphore_signal(barrier, inc=1, device_id={"dp": peer}, device_id_type=MESH)
        return carry

    lax.fori_loop(1, n_ctx, greet_ctx, 0)
    lax.fori_loop(1, n_dp, greet_dp, 0)

    loads = []
    for source, target in (
        (x_hbm.at[0], raw.at[0]),
        (g_hbm.at[0], raw.at[1]),
        (first_hbm, w_first),
        (turn_hbm, t_turn),
        (second_hbm, w_second),
        (last_hbm, w_last),
        (n_hbm.at[0], raw.at[2]),
        (master_hbm, state_in.at[0]),
        (one_hbm, state_in.at[1]),
        (two_hbm, state_in.at[2]),
    ):
        copy = pltpu.make_async_copy(source, target, local_sem.at[len(loads)])
        copy.start()
        loads.append(copy)

    def regroup(which):
        for i in range(rows_block):
            part = raw[which, :, i * cols : (i + 1) * cols].astype(F32)
            for lane in range(cols // LANES):
                mixed[lane, i * channels : (i + 1) * channels, :] = part[
                    :, lane * LANES : (lane + 1) * LANES
                ]
        for c in range(channels):
            for lane in range(cols // LANES):
                block_send[which, c, :, lane * LANES : (lane + 1) * LANES] = mixed[
                    lane, pl.ds(c, rows_block, stride=channels), :
                ].astype(BF16)

    def send_block(which, ch):
        def one(i, carry):
            peer = lax.rem(me + i, n_ctx)
            pltpu.make_async_remote_copy(
                src_ref=block_send.at[which, peer * owned + ch],
                dst_ref=block_recv.at[which, ch, me],
                send_sem=block_ssem.at[which, ch],
                recv_sem=block_rsem.at[which, ch],
                device_id={"ctx": peer},
                device_id_type=MESH,
            ).start()
            return carry

        lax.fori_loop(1, n_ctx, one, 0)
        block_recv[which, ch, me] = block_send[which, me * owned + ch]

    def wait_bytes(ref, count, sem):
        part = ref.at[pl.ds(0, count)]
        pltpu.make_async_copy(part, part, sem).wait()

    def wait_block(which, ch):
        wait_bytes(block_recv.at[which, ch], n_ctx - 1, block_rsem.at[which, ch])
        return block_recv[which, ch].reshape(rows, cols)

    def spectrum(block):
        return forward(block, t_first, t_turn, t_forward)

    loads[0].wait()
    regroup(0)
    pl.semaphore_wait(barrier, n_ctx + n_dp - 2)
    send_block(0, 0)
    loads[1].wait()
    regroup(1)
    send_block(1, 0)
    for copy in loads[2:]:
        copy.wait()
    t_first[: 2 * rows], t_first[2 * rows :] = halves(w_first[...])
    t_last[:rows], t_last[rows:] = halves(w_last[...])
    low_cols, high_cols = slice(0, cols), slice(cols, 2 * cols)
    for part, (cosine, sine) in enumerate(zip(halves(w_second[0]), halves(w_second[1]))):
        for table, upper, lower in ((t_forward, -sine, sine), (t_back, sine, -sine)):
            table[part, low_cols, low_cols] = cosine
            table[part, low_cols, high_cols] = upper
            table[part, high_cols, low_cols] = lower
            table[part, high_cols, high_cols] = cosine
    regroup(2)

    def fold_row(i, carry):
        span = pl.ds(pl.multiple_of(i * cols, LANES), cols)
        for which in range(3):
            for ch in range(owned):
                state[which, ch, pl.ds(i, 1), :] = state_in[which, ch : ch + 1, span]
        return carry

    lax.fori_loop(0, rows_own, fold_row, 0, unroll=4)

    def keep(values):
        spec[0], spec[1] = values

    def gradient(ch):
        g_block = wait_block(1, ch)
        send_block(*((1, ch + 1) if ch + 1 < owned else (2, 0)))
        g_re, g_im = spectrum(g_block)
        x_re, x_im = spec[0], spec[1]
        total = inverse(
            x_re * g_re + x_im * g_im, x_re * g_im - x_im * g_re, t_turn, t_back, t_last
        ).reshape(n_dp, rows_own, cols)
        partial[ch] = total
        grad_send[ch] = total.astype(BF16)

        def one(i, carry):
            peer = lax.rem(me_dp + i, n_dp)
            pltpu.make_async_remote_copy(
                src_ref=grad_send.at[ch, peer],
                dst_ref=grad_recv.at[ch, i - 1],
                send_sem=grad_ssem.at[ch],
                recv_sem=grad_rsem.at[ch],
                device_id={"dp": peer},
                device_id_type=MESH,
            ).start()
            return carry

        lax.fori_loop(1, n_dp, one, 0)

    def update(ch):
        wait_bytes(grad_recv.at[ch], n_dp - 1, grad_rsem.at[ch])
        grad = partial[ch, me_dp]
        for i in range(n_dp - 1):
            grad = grad + grad_recv[ch, i].astype(F32)
        master = state[0, ch]
        new_one = 0.9 * state[1, ch] + 0.1 * grad
        new_two = 0.999 * state[2, ch] + 0.001 * grad * grad
        first_hat = new_one / (1.0 - 0.9**10)
        second_hat = new_two / (1.0 - 0.999**10)
        new_master = master - 0.01 * (first_hat / (jnp.sqrt(second_hat) + 1e-08) + 0.1 * master)
        filt[ch, me_dp] = new_master.astype(BF16)

        def one(i, carry):
            peer = lax.rem(me_dp + i, n_dp)
            pltpu.make_async_remote_copy(
                src_ref=filt.at[ch, me_dp],
                dst_ref=filt.at[ch, me_dp],
                send_sem=filt_ssem.at[ch],
                recv_sem=filt_rsem.at[ch],
                device_id={"dp": peer},
                device_id_type=MESH,
            ).start()
            return carry

        lax.fori_loop(1, n_dp, one, 0)
        for which, value in enumerate((new_master, new_one, new_two)):
            state[which, ch] = value

        def flat_row(i, carry):
            span = pl.ds(pl.multiple_of(i * cols, LANES), cols)
            for which in range(3):
                state_out[which, ch : ch + 1, span] = state[which, ch, pl.ds(i, 1), :]
            return carry

        lax.fori_loop(0, rows_own, flat_row, 0, unroll=8)

    def product(ch):
        wait_bytes(filt.at[ch], n_dp - 1, filt_rsem.at[ch])
        f_re, f_im = spectrum(filt[ch].reshape(rows, cols))
        x_re, x_im = spec[0], spec[1]
        keep((x_re * f_re - x_im * f_im, x_re * f_im + x_im * f_re))

    def finish(ch):
        result = inverse(spec[0], spec[1], t_turn, t_back, t_last)
        out_send[ch] = result.astype(BF16).reshape(n_ctx, rows_block, cols)

        def one(i, carry):
            peer = lax.rem(me + i, n_ctx)
            pltpu.make_async_remote_copy(
                src_ref=out_send.at[ch, peer],
                dst_ref=out_recv.at[me * owned + ch],
                send_sem=out_ssem.at[ch],
                recv_sem=out_rsem.at[ch],
                device_id={"ctx": peer},
                device_id_type=MESH,
            ).start()
            return carry

        lax.fori_loop(1, n_ctx, one, 0)
        copy = pltpu.make_async_copy(
            out_send.at[ch, me], out_recv.at[me * owned + ch], local_sem.at[ch]
        )
        copy.start()
        stores.append(copy)

    stores = []
    for ch in range(owned):
        x_block = wait_block(0, ch)
        if ch + 1 < owned:
            send_block(0, ch + 1)
        keep(spectrum(x_block))
        if ch:
            update(ch - 1)
        gradient(ch)
    final = owned - 1
    for ch in range(final):
        send_block(2, ch + 1)
        keep(spectrum(wait_block(2, ch)))
        product(ch)
        if ch == final - 1:
            update(final)
        finish(ch)
    if not final:
        update(final)
    keep(spectrum(wait_block(2, final)))
    product(final)
    for which, target in enumerate((master_out, one_out, two_out)):
        copy = pltpu.make_async_copy(state_out.at[which], target, store_sem.at[which])
        copy.start()
        stores.append(copy)
    finish(final)
    for ch in range(owned):
        for which in range(3):
            wait_bytes(block_send.at[which], n_ctx - 1, block_ssem.at[which, ch])
        wait_bytes(grad_send.at[ch], n_dp - 1, grad_ssem.at[ch])
        wait_bytes(filt.at[ch], n_dp - 1, filt_ssem.at[ch])
        wait_bytes(out_send.at[ch], n_ctx - 1, out_ssem.at[ch])
    for ch in range(owned):
        wait_bytes(out_recv, n_ctx - 1, out_rsem.at[ch])
    for copy in stores:
        copy.wait()


def settle(
    master, one, two, blocks, master_out, one_out, two_out, next_out, held, block, mixed, flat, sems
):
    channels, rows_block, cols = block.shape
    load = pltpu.make_async_copy(blocks, block, sems.at[0])
    load.start()
    loads = [
        pltpu.make_async_copy(source, held.at[i], sems.at[1 + i])
        for i, source in enumerate((master, one, two))
    ]
    stores = [
        pltpu.make_async_copy(held.at[i], target, sems.at[4 + i])
        for i, target in enumerate((master_out, one_out, two_out))
    ]
    for copy in loads:
        copy.start()
    load.wait()
    for c in range(channels):
        part = block[c].astype(F32)
        for lane in range(cols // LANES):
            mixed[lane, c * rows_block : (c + 1) * rows_block, :] = part[
                :, lane * LANES : (lane + 1) * LANES
            ]
    for before, after in zip(loads, stores):
        before.wait()
        after.start()
    for i in range(rows_block):
        for lane in range(cols // LANES):
            start = i * cols + lane * LANES
            flat[:, start : start + LANES] = mixed[
                lane, pl.ds(i, channels, stride=rows_block), :
            ].astype(BF16)
    store = pltpu.make_async_copy(flat, next_out.at[0], sems.at[7])
    store.start()
    for copy in stores:
        copy.wait()
    store.wait()


def local(n_dp, n_ctx, inputs, out_grad, master, moment_one, moment_two, next_inputs):
    channels, span = inputs.shape[1:]
    owned, taps_own = master.shape
    length = n_ctx * span
    cols = min(256, span // 16)
    rows = length // cols
    rows_block, rows_own = span // cols, taps_own // cols
    table_list = tables(rows, cols)
    dma = pltpu.SemaphoreType.DMA
    vmem = pltpu.VMEM
    anywhere = pl.BlockSpec(memory_space=pltpu.HBM)
    macs = 12 * owned * length * (rows + 2 * cols) * 3
    results = pl.pallas_call(
        functools.partial(layer, n_dp, n_ctx),
        name="layer",
        out_shape=(
            jax.ShapeDtypeStruct(master.shape, F32),
            jax.ShapeDtypeStruct(master.shape, F32),
            jax.ShapeDtypeStruct(master.shape, F32),
            jax.ShapeDtypeStruct((channels, rows_block, cols), BF16),
        ),
        in_specs=[anywhere] * 10,
        out_specs=[anywhere] * 4,
        scratch_shapes=[
            vmem((3, channels, span), BF16),
            vmem((cols // LANES, channels * rows_block, LANES), F32),
            vmem((3, channels, rows_block, cols), BF16),
            vmem((3, owned, n_ctx, rows_block, cols), BF16),
            *[vmem(table.shape, F32) for table in table_list],
            vmem((4 * rows, rows), BF16),
            vmem((2, 2 * cols, 2 * cols), BF16),
            vmem((2, 2 * cols, 2 * cols), BF16),
            vmem((2 * rows, 2 * rows), BF16),
            vmem((3, owned, taps_own), F32),
            vmem((3, owned, rows_own, cols), F32),
            vmem((3, owned, taps_own), F32),
            vmem((2, rows, cols), F32),
            vmem((owned, n_dp, rows_own, cols), F32),
            vmem((owned, n_dp, rows_own, cols), BF16),
            vmem((owned, n_dp - 1, rows_own, cols), BF16),
            vmem((owned, n_dp, rows_own, cols), BF16),
            vmem((owned, n_ctx, rows_block, cols), BF16),
            dma((10,)),
            dma((3,)),
            dma((3, owned)),
            dma((3, owned)),
            dma((owned,)),
            dma((owned,)),
            dma((owned,)),
            dma((owned,)),
            dma((owned,)),
            dma((owned,)),
        ],
        compiler_params=pltpu.CompilerParams(
            collective_id=0, has_side_effects=True, vmem_limit_bytes=56 * 1024 * 1024
        ),
        cost_estimate=pl.CostEstimate(
            flops=2 * macs, bytes_accessed=8 * 1024 * 1024, transcendentals=0
        ),
    )(inputs, out_grad, master, moment_one, moment_two, next_inputs, *table_list)
    return pl.pallas_call(
        settle,
        name="settle",
        out_shape=(
            jax.ShapeDtypeStruct(master.shape, F32),
            jax.ShapeDtypeStruct(master.shape, F32),
            jax.ShapeDtypeStruct(master.shape, F32),
            jax.ShapeDtypeStruct(inputs.shape, BF16),
        ),
        in_specs=[anywhere] * 4,
        out_specs=[anywhere] * 4,
        scratch_shapes=[
            vmem((3, owned, taps_own), F32),
            vmem((channels, rows_block, cols), BF16),
            vmem((cols // LANES, channels * rows_block, LANES), F32),
            vmem((channels, span), BF16),
            dma((8,)),
        ],
        compiler_params=pltpu.CompilerParams(vmem_limit_bytes=56 * 1024 * 1024),
    )(*results)


def solution(mesh):
    return jax.shard_map(
        functools.partial(local, mesh.shape["dp"], mesh.shape["ctx"]),
        mesh=mesh,
        in_specs=(
            P("dp", None, "ctx"),
            P("dp", None, "ctx"),
            P("ctx", "dp"),
            P("ctx", "dp"),
            P("ctx", "dp"),
            P("dp", None, "ctx"),
        ),
        out_specs=(P("ctx", "dp"), P("ctx", "dp"), P("ctx", "dp"), P("dp", None, "ctx")),
        check_vma=False,
    )
```

```python
import functools

import jax
import jax.numpy as jnp
import numpy as np
from jax import lax
from jax.experimental import pallas as pl
from jax.experimental.pallas import tpu as pltpu
from jax.sharding import PartitionSpec as P

F32 = jnp.float32
BF16 = jnp.bfloat16
LANES = 128
MESH = pl.DeviceIdType.MESH


def tables(rows, cols):
    length = rows * cols
    shifted = np.arange(rows, dtype=np.float64) + 0.25
    first = 2.0 * np.pi * np.outer(shifted, np.arange(rows)) / rows
    turn = 2.0 * np.pi * np.outer(shifted, np.arange(cols)) / length
    second = 2.0 * np.pi * (np.outer(np.arange(cols), np.arange(cols)) % cols) / cols
    return tuple(
        table.astype(np.float32)
        for table in (
            np.concatenate([np.cos(first), -np.sin(first)], 0),
            np.stack([np.cos(turn), -np.sin(turn)]),
            np.stack([np.cos(second), np.sin(second)]),
            np.concatenate([np.cos(first).T, -np.sin(first).T], 1) / length,
        )
    )


def dot(left, right):
    return jnp.dot(left, right, preferred_element_type=F32)


def halves(value):
    high = value.astype(BF16)
    return high, (value - high.astype(F32)).astype(BF16)


def thrice(value, table):
    rows = value.shape[0]
    high, low = halves(value)
    both = dot(jnp.concatenate([high, low], axis=0), table[0])
    return both[:rows] + (both[rows:] + dot(high, table[1]))


def columns(real, imag, t_second, back):
    common = thrice(real + imag, t_second.at[0])
    if back:
        return common - thrice(imag, t_second.at[2]), common + thrice(real, t_second.at[1])
    return common + thrice(imag, t_second.at[1]), common - thrice(real, t_second.at[2])


def forward(block, t_first, t_turn, t_second):
    rows = block.shape[0]
    mixed = dot(t_first[...], block)
    real = mixed[:rows] + mixed[2 * rows : 3 * rows]
    imag = mixed[rows : 2 * rows] + mixed[3 * rows :]
    turn_re, turn_im = t_turn[0], t_turn[1]
    return columns(
        real * turn_re - imag * turn_im, real * turn_im + imag * turn_re, t_second, False
    )


def inverse(real, imag, t_turn, t_second, t_last):
    rows = real.shape[0]
    real, imag = columns(real, imag, t_second, True)
    turn_re, turn_im = t_turn[0], t_turn[1]
    high, low = halves(
        jnp.concatenate([real * turn_re + imag * turn_im, imag * turn_re - real * turn_im], axis=0)
    )
    both = dot(t_last[...], high)
    return both[:rows] + (both[rows:] + dot(t_last[:rows], low))


def layer(
    n_dp,
    n_ctx,
    x_hbm,
    g_hbm,
    master_hbm,
    one_hbm,
    two_hbm,
    n_hbm,
    first_hbm,
    turn_hbm,
    second_hbm,
    last_hbm,
    master_out,
    one_out,
    two_out,
    out_recv,
    raw,
    mixed,
    block_send,
    block_recv,
    w_first,
    t_turn,
    w_second,
    w_last,
    t_first,
    t_second,
    t_last,
    state_in,
    state,
    state_out,
    spec,
    partial,
    grad_send,
    grad_recv,
    filt,
    out_send,
    local_sem,
    store_sem,
    block_ssem,
    block_rsem,
    grad_ssem,
    grad_rsem,
    filt_ssem,
    filt_rsem,
    out_ssem,
    out_rsem,
):
    me_dp = lax.axis_index("dp")
    me = lax.axis_index("ctx")
    channels = raw.shape[1]
    owned = block_recv.shape[1]
    rows_block, cols = block_send.shape[2:]
    rows = n_ctx * rows_block
    rows_own = filt.shape[2]

    barrier = pltpu.get_barrier_semaphore()

    def partner(i):
        offset = n_ctx // 2 + lax.div(i, 2) * (2 * lax.rem(i, 2) - 1)
        return lax.rem(me + offset, n_ctx)

    def greet_ctx(i, carry):
        peer = lax.rem(me + i, n_ctx)
        pl.semaphore_signal(barrier, inc=1, device_id={"ctx": peer}, device_id_type=MESH)
        return carry

    def greet_dp(i, carry):
        peer = lax.rem(me_dp + i, n_dp)
        pl.semaphore_signal(barrier, inc=1, device_id={"dp": peer}, device_id_type=MESH)
        return carry

    lax.fori_loop(1, n_ctx, greet_ctx, 0)
    lax.fori_loop(1, n_dp, greet_dp, 0)

    loads = []
    for source, target in (
        (x_hbm.at[0], raw.at[0]),
        (g_hbm.at[0], raw.at[1]),
        (first_hbm, w_first),
        (turn_hbm, t_turn),
        (second_hbm, w_second),
        (last_hbm, w_last),
        (n_hbm.at[0], raw.at[2]),
        (master_hbm, state_in.at[0]),
        (one_hbm, state_in.at[1]),
        (two_hbm, state_in.at[2]),
    ):
        copy = pltpu.make_async_copy(source, target, local_sem.at[len(loads)])
        copy.start()
        loads.append(copy)

    def regroup(which):
        for i in range(rows_block):
            part = raw[which, :, i * cols : (i + 1) * cols].astype(F32)
            for lane in range(cols // LANES):
                mixed[lane, i * channels : (i + 1) * channels, :] = part[
                    :, lane * LANES : (lane + 1) * LANES
                ]
        for c in range(channels):
            for lane in range(cols // LANES):
                block_send[which, c, :, lane * LANES : (lane + 1) * LANES] = mixed[
                    lane, pl.ds(c, rows_block, stride=channels), :
                ].astype(BF16)

    def send_block(which, ch):
        def one(i, carry):
            peer = partner(i)
            pltpu.make_async_remote_copy(
                src_ref=block_send.at[which, peer * owned + ch],
                dst_ref=block_recv.at[which, ch, me],
                send_sem=block_ssem.at[which, ch],
                recv_sem=block_rsem.at[which, ch],
                device_id={"ctx": peer},
                device_id_type=MESH,
            ).start()
            return carry

        lax.fori_loop(1, n_ctx, one, 0)
        block_recv[which, ch, me] = block_send[which, me * owned + ch]

    def wait_bytes(ref, count, sem):
        part = ref.at[pl.ds(0, count)]
        pltpu.make_async_copy(part, part, sem).wait()

    def wait_block(which, ch):
        wait_bytes(block_recv.at[which, ch], n_ctx - 1, block_rsem.at[which, ch])
        return block_recv[which, ch].reshape(rows, cols)

    def spectrum(block):
        return forward(block, t_first, t_turn, t_second)

    loads[0].wait()
    regroup(0)
    pl.semaphore_wait(barrier, n_ctx + n_dp - 2)
    send_block(0, 0)
    loads[1].wait()
    regroup(1)
    send_block(1, 0)
    for copy in loads[2:]:
        copy.wait()
    t_first[: 2 * rows], t_first[2 * rows :] = halves(w_first[...])
    t_last[:rows], t_last[rows:] = halves(w_last[...])
    cosine, sine = w_second[0], w_second[1]
    for i, table in enumerate((cosine, sine - cosine, sine + cosine)):
        t_second[i, 0], t_second[i, 1] = halves(table)
    regroup(2)

    def fold_row(i, carry):
        span = pl.ds(pl.multiple_of(i * cols, LANES), cols)
        for which in range(3):
            for ch in range(owned):
                state[which, ch, pl.ds(i, 1), :] = state_in[which, ch : ch + 1, span]
        return carry

    lax.fori_loop(0, rows_own, fold_row, 0, unroll=4)

    def keep(values):
        spec[0], spec[1] = values

    def gradient(ch):
        g_block = wait_block(1, ch)
        send_block(*((1, ch + 1) if ch + 1 < owned else (2, 0)))
        g_re, g_im = spectrum(g_block)
        x_re, x_im = spec[0], spec[1]
        total = inverse(
            x_re * g_re + x_im * g_im, x_re * g_im - x_im * g_re, t_turn, t_second, t_last
        ).reshape(n_dp, rows_own, cols)
        partial[ch] = total
        grad_send[ch] = total.astype(BF16)

        def one(i, carry):
            peer = lax.rem(me_dp + i, n_dp)
            pltpu.make_async_remote_copy(
                src_ref=grad_send.at[ch, peer],
                dst_ref=grad_recv.at[ch, i - 1],
                send_sem=grad_ssem.at[ch],
                recv_sem=grad_rsem.at[ch],
                device_id={"dp": peer},
                device_id_type=MESH,
            ).start()
            return carry

        lax.fori_loop(1, n_dp, one, 0)

    def update(ch):
        wait_bytes(grad_recv.at[ch], n_dp - 1, grad_rsem.at[ch])
        grad = partial[ch, me_dp]
        for i in range(n_dp - 1):
            grad = grad + grad_recv[ch, i].astype(F32)
        master = state[0, ch]
        new_one = 0.9 * state[1, ch] + 0.1 * grad
        new_two = 0.999 * state[2, ch] + 0.001 * grad * grad
        first_hat = new_one / (1.0 - 0.9**10)
        second_hat = new_two / (1.0 - 0.999**10)
        new_master = master - 0.01 * (first_hat / (jnp.sqrt(second_hat) + 1e-08) + 0.1 * master)
        filt[ch, me_dp] = new_master.astype(BF16)

        def one(i, carry):
            peer = lax.rem(me_dp + i, n_dp)
            pltpu.make_async_remote_copy(
                src_ref=filt.at[ch, me_dp],
                dst_ref=filt.at[ch, me_dp],
                send_sem=filt_ssem.at[ch],
                recv_sem=filt_rsem.at[ch],
                device_id={"dp": peer},
                device_id_type=MESH,
            ).start()
            return carry

        lax.fori_loop(1, n_dp, one, 0)
        for which, value in enumerate((new_master, new_one, new_two)):
            state[which, ch] = value

        def flat_row(i, carry):
            span = pl.ds(pl.multiple_of(i * cols, LANES), cols)
            for which in range(3):
                state_out[which, ch : ch + 1, span] = state[which, ch, pl.ds(i, 1), :]
            return carry

        lax.fori_loop(0, rows_own, flat_row, 0, unroll=8)

    def product(ch):
        wait_bytes(filt.at[ch], n_dp - 1, filt_rsem.at[ch])
        f_re, f_im = spectrum(filt[ch].reshape(rows, cols))
        x_re, x_im = spec[0], spec[1]
        keep((x_re * f_re - x_im * f_im, x_re * f_im + x_im * f_re))

    def finish(ch):
        result = inverse(spec[0], spec[1], t_turn, t_second, t_last)
        out_send[ch] = result.astype(BF16).reshape(n_ctx, rows_block, cols)

        def one(i, carry):
            peer = partner(i)
            pltpu.make_async_remote_copy(
                src_ref=out_send.at[ch, peer],
                dst_ref=out_recv.at[me * owned + ch],
                send_sem=out_ssem.at[ch],
                recv_sem=out_rsem.at[ch],
                device_id={"ctx": peer},
                device_id_type=MESH,
            ).start()
            return carry

        lax.fori_loop(1, n_ctx, one, 0)
        copy = pltpu.make_async_copy(
            out_send.at[ch, me], out_recv.at[me * owned + ch], local_sem.at[ch]
        )
        copy.start()
        stores.append(copy)

    stores = []
    for ch in range(owned):
        x_block = wait_block(0, ch)
        if ch + 1 < owned:
            send_block(0, ch + 1)
        keep(spectrum(x_block))
        if ch:
            update(ch - 1)
        gradient(ch)
    final = owned - 1
    for ch in range(final):
        send_block(2, ch + 1)
        keep(spectrum(wait_block(2, ch)))
        product(ch)
        if ch == final - 1:
            update(final)
        finish(ch)
    if not final:
        update(final)
    keep(spectrum(wait_block(2, final)))
    product(final)
    for which, target in enumerate((master_out, one_out, two_out)):
        copy = pltpu.make_async_copy(state_out.at[which], target, store_sem.at[which])
        copy.start()
        stores.append(copy)
    finish(final)
    for ch in range(owned):
        for which in range(3):
            wait_bytes(block_send.at[which], n_ctx - 1, block_ssem.at[which, ch])
        wait_bytes(grad_send.at[ch], n_dp - 1, grad_ssem.at[ch])
        wait_bytes(filt.at[ch], n_dp - 1, filt_ssem.at[ch])
        wait_bytes(out_send.at[ch], n_ctx - 1, out_ssem.at[ch])
    for ch in range(owned):
        wait_bytes(out_recv, n_ctx - 1, out_rsem.at[ch])
    for copy in stores:
        copy.wait()


def settle(
    master, one, two, blocks, master_out, one_out, two_out, next_out, held, block, mixed, flat, sems
):
    channels, rows_block, cols = block.shape
    load = pltpu.make_async_copy(blocks, block, sems.at[0])
    load.start()
    loads = [
        pltpu.make_async_copy(source, held.at[i], sems.at[1 + i])
        for i, source in enumerate((master, one, two))
    ]
    stores = [
        pltpu.make_async_copy(held.at[i], target, sems.at[4 + i])
        for i, target in enumerate((master_out, one_out, two_out))
    ]
    for copy in loads:
        copy.start()
    load.wait()
    for c in range(channels):
        part = block[c].astype(F32)
        for lane in range(cols // LANES):
            mixed[lane, c * rows_block : (c + 1) * rows_block, :] = part[
                :, lane * LANES : (lane + 1) * LANES
            ]
    for before, after in zip(loads, stores):
        before.wait()
        after.start()
    for i in range(rows_block):
        for lane in range(cols // LANES):
            start = i * cols + lane * LANES
            flat[:, start : start + LANES] = mixed[
                lane, pl.ds(i, channels, stride=rows_block), :
            ].astype(BF16)
    store = pltpu.make_async_copy(flat, next_out.at[0], sems.at[7])
    store.start()
    for copy in stores:
        copy.wait()
    store.wait()


def local(n_dp, n_ctx, inputs, out_grad, master, moment_one, moment_two, next_inputs):
    channels, span = inputs.shape[1:]
    owned, taps_own = master.shape
    length = n_ctx * span
    cols = min(256, span // 16)
    rows = length // cols
    rows_block, rows_own = span // cols, taps_own // cols
    table_list = tables(rows, cols)
    dma = pltpu.SemaphoreType.DMA
    vmem = pltpu.VMEM
    anywhere = pl.BlockSpec(memory_space=pltpu.HBM)
    macs = 12 * owned * length * (rows + 2 * cols) * 3
    results = pl.pallas_call(
        functools.partial(layer, n_dp, n_ctx),
        name="layer",
        out_shape=(
            jax.ShapeDtypeStruct(master.shape, F32),
            jax.ShapeDtypeStruct(master.shape, F32),
            jax.ShapeDtypeStruct(master.shape, F32),
            jax.ShapeDtypeStruct((channels, rows_block, cols), BF16),
        ),
        in_specs=[anywhere] * 10,
        out_specs=[anywhere] * 4,
        scratch_shapes=[
            vmem((3, channels, span), BF16),
            vmem((cols // LANES, channels * rows_block, LANES), F32),
            vmem((3, channels, rows_block, cols), BF16),
            vmem((3, owned, n_ctx, rows_block, cols), BF16),
            *[vmem(table.shape, F32) for table in table_list],
            vmem((4 * rows, rows), BF16),
            vmem((3, 2, cols, cols), BF16),
            vmem((2 * rows, 2 * rows), BF16),
            vmem((3, owned, taps_own), F32),
            vmem((3, owned, rows_own, cols), F32),
            vmem((3, owned, taps_own), F32),
            vmem((2, rows, cols), F32),
            vmem((owned, n_dp, rows_own, cols), F32),
            vmem((owned, n_dp, rows_own, cols), BF16),
            vmem((owned, n_dp - 1, rows_own, cols), BF16),
            vmem((owned, n_dp, rows_own, cols), BF16),
            vmem((owned, n_ctx, rows_block, cols), BF16),
            dma((10,)),
            dma((3,)),
            dma((3, owned)),
            dma((3, owned)),
            dma((owned,)),
            dma((owned,)),
            dma((owned,)),
            dma((owned,)),
            dma((owned,)),
            dma((owned,)),
        ],
        compiler_params=pltpu.CompilerParams(
            collective_id=0, has_side_effects=True, vmem_limit_bytes=56 * 1024 * 1024
        ),
        cost_estimate=pl.CostEstimate(
            flops=2 * macs, bytes_accessed=8 * 1024 * 1024, transcendentals=0
        ),
    )(inputs, out_grad, master, moment_one, moment_two, next_inputs, *table_list)
    return pl.pallas_call(
        settle,
        name="settle",
        out_shape=(
            jax.ShapeDtypeStruct(master.shape, F32),
            jax.ShapeDtypeStruct(master.shape, F32),
            jax.ShapeDtypeStruct(master.shape, F32),
            jax.ShapeDtypeStruct(inputs.shape, BF16),
        ),
        in_specs=[anywhere] * 4,
        out_specs=[anywhere] * 4,
        scratch_shapes=[
            vmem((3, owned, taps_own), F32),
            vmem((channels, rows_block, cols), BF16),
            vmem((cols // LANES, channels * rows_block, LANES), F32),
            vmem((channels, span), BF16),
            dma((8,)),
        ],
        compiler_params=pltpu.CompilerParams(vmem_limit_bytes=56 * 1024 * 1024),
    )(*results)


def solution(mesh):
    return jax.shard_map(
        functools.partial(local, mesh.shape["dp"], mesh.shape["ctx"]),
        mesh=mesh,
        in_specs=(
            P("dp", None, "ctx"),
            P("dp", None, "ctx"),
            P("ctx", "dp"),
            P("ctx", "dp"),
            P("ctx", "dp"),
            P("dp", None, "ctx"),
        ),
        out_specs=(P("ctx", "dp"), P("ctx", "dp"), P("ctx", "dp"), P("dp", None, "ctx")),
        check_vma=False,
    )
```
